128 devices in a mesh: dom: 32 (over z, x_lo, y), edge: 4 (over x_hi, core).
Axes of the slice: x: 4 (x_hi: 2, x_lo: 2; x = x_hi * 2 + x_lo), y: 4, z: 4, core: 2. Of those that a mesh axis runs over, the one named last changes fastest.
Arguments:
- left_table: float32 [65536, 256], P(('dom', 'edge')), may hold values from -2.4 to 2.4
- left_state: float32 [65536], P(('dom', 'edge')), may hold values from 0.02 to 0.2
- right_table: float32 [65536, 256], P(('dom', 'edge')), may hold values from -2.4 to 2.4
- right_state: float32 [65536], P(('dom', 'edge')), may hold values from 0.02 to 0.2
- relations: float32 [2048, 256], replicated, may hold values from -2.4 to 2.4
- relation_state: float32 [2048], replicated, may hold values from 0.02 to 0.2
- src_rows: int32 [2, 131072], P(None, ('dom', 'edge')), may hold values from 0 to 2047
- dst_rows: int32 [2, 131072], P(None, ('dom', 'edge')), may hold values from 0 to 2047
- rel_ids: int32 [2, 131072], P(None, ('dom', 'edge')), may hold values from 0 to 2047
- neg_rows: int32 [2, 32768], P(None, ('dom', 'edge')), may hold values from 0 to 2047
Outputs:
- left_new: float32 [65536, 256], P(('dom', 'edge'))
- left_state_new: float32 [65536], P(('dom', 'edge'))
- right_new: float32 [65536, 256], P(('dom', 'edge'))
- right_state_new: float32 [65536], P(('dom', 'edge'))
- relations_new: float32 [2048, 256], replicated
- relation_state_new: float32 [2048], replicated
The draws below stay inside these ranges and needn't reach their ends.
All inputs are finite; a program needn't handle non-finite values.
Results may differ from the reference program's by a relative error of at most 0.0019.
Values may be sent and summed in bfloat16 or wider, within the bound.
A program may use at most 64 MiB of HBM per device.

```python
import math
import jax
import jax.numpy as jnp
from jax import lax

DIM = 256
REL = 2048
NEG = 256
STEPS = 2
EDGES = 1024
SLAB = 2048
ENT = 65536
ALL_EDGES = 131072
ALL_NEG = 32768
N_DOM = 32
N_EDGE = 4


def draw_rel_ids(key, part):
    key = jax.random.fold_in(key, 5)
    columns = jnp.arange(ALL_EDGES, dtype=jnp.int32)
    result = jax.random.randint(key, (STEPS, ALL_EDGES), 0, REL, dtype=jnp.int32)
    result = jnp.where(columns[None, :] == ALL_EDGES - 1, REL - 1, result)
    result = jnp.where(columns[None, :] == 0, 0, result)
    return result.astype(jnp.int32)


def set_ends(values, key, low, top_value):
    index_at = [jax.random.randint(jax.random.fold_in(key, axis), (), 0, length) for axis, length in enumerate(values.shape)]
    longest = values.shape.index(max(values.shape))
    next_to = index_at[:longest] + [(index_at[longest] + 1) % values.shape[longest]] + index_at[longest + 1:]
    return values.at[tuple(index_at)].set(low).at[tuple(next_to)].set(top_value)


def shard_levels(stream_key, shape, cuts, least, high):
    def one(position, parts):
        heights = jax.random.uniform(jax.random.fold_in(jax.random.fold_in(stream_key, 6), position), (parts,), jnp.float32, least / len(cuts), high / len(cuts))
        return jnp.repeat(jnp.exp(heights), shape[position] // parts).reshape((-1,) + (1,) * (len(shape) - position - 1))

    loudness = one(*cuts[0])
    for cut in cuts[1:]:
        loudness = loudness * one(*cut)
    return loudness


def normal_values(key, dims, width, reach, cuts=(), kind=jnp.bfloat16):
    factor_of = shard_levels(key, dims, cuts, -0.22, 0.18) if cuts else 1.0
    drawn = jax.random.normal(key, dims, jnp.float32) * width * factor_of
    return jnp.minimum(jnp.maximum(drawn, -reach), reach).astype(kind)


def setup_inputs(seed: int = 0) -> dict:
    seeds = jax.random.split(jax.random.key(seed), 11)
    return {
        "left_table": normal_values(seeds[0], (ENT, DIM), 0.4, 2.4, ((0, 128),), jnp.float32),
        "left_state": jnp.clip(jnp.exp(math.log(0.2) - 2.3025851 * jax.random.uniform(seeds[1], (ENT,), jnp.float32) ** shard_levels(seeds[1], (ENT,), ((0, 128),), -0.2, 0.2)), 0.02, 0.2),
        "right_table": normal_values(seeds[2], (ENT, DIM), 0.4, 2.4, ((0, 128),), jnp.float32),
        "right_state": jnp.clip(jnp.exp(math.log(0.2) - 2.3025851 * jax.random.uniform(seeds[3], (ENT,), jnp.float32) ** shard_levels(seeds[3], (ENT,), ((0, 128),), -0.2, 0.2)), 0.02, 0.2),
        "relations": normal_values(seeds[4], (REL, DIM), 0.4, 2.4, (), jnp.float32),
        "relation_state": jnp.clip(jnp.exp(jax.random.uniform(seeds[5], (REL,), jnp.float32, math.log(0.02), math.log(0.2))), 0.02, 0.2),
        "src_rows": set_ends(jax.random.randint(seeds[6], (STEPS, ALL_EDGES), 0, SLAB), jax.random.fold_in(seeds[6], 1), 0, SLAB - 1).astype(jnp.int32),
        "dst_rows": set_ends(jax.random.randint(seeds[7], (STEPS, ALL_EDGES), 0, SLAB), jax.random.fold_in(seeds[7], 1), 0, SLAB - 1).astype(jnp.int32),
        "rel_ids": draw_rel_ids(jax.random.fold_in(seeds[10], 71), 0),
        "neg_rows": set_ends(jax.random.randint(seeds[9], (STEPS, ALL_NEG), 0, SLAB), jax.random.fold_in(seeds[9], 1), 0, SLAB - 1).astype(jnp.int32),
    }


learn_rate = 0.1
neg_weight = 0.0625

def adagrad(table, state, grad):
    state = state + lax.optimization_barrier(jnp.mean(grad * grad, axis=-1))
    return (table - learn_rate * grad / jnp.sqrt(state)[:, None], state)

def reference(left_table, left_state, right_table, right_state, relations, relation_state, src_rows, dst_rows, rel_ids, neg_rows):
    half_dim = DIM // 2
    device_count = N_DOM * N_EDGE
    part_base = (jnp.arange(device_count, dtype=jnp.int32) // N_EDGE * SLAB)[:, None]
    highest = lax.Precision.HIGHEST
    for bucket in range(STEPS):
        right_table = jnp.roll(right_table, SLAB, axis=0)
        right_state = jnp.roll(right_state, SLAB, axis=0)
        left_b = left_table.astype(jnp.bfloat16)
        right_b = right_table.astype(jnp.bfloat16)
        relations_b = relations.astype(jnp.bfloat16)
        src_index = src_rows[bucket].reshape(device_count, EDGES) + part_base
        dst_index = dst_rows[bucket].reshape(device_count, EDGES) + part_base
        neg_index = neg_rows[bucket].reshape(device_count, NEG) + part_base
        rel_index = rel_ids[bucket].reshape(device_count, EDGES)
        source = left_b[src_index].astype(jnp.float32)
        target = right_b[dst_index].astype(jnp.float32)
        negatives = right_b[neg_index].astype(jnp.float32)
        relation = relations_b[rel_index].astype(jnp.float32)
        src_re, src_im = (source[..., :half_dim], source[..., half_dim:])
        rel_re, rel_im = (relation[..., :half_dim], relation[..., half_dim:])
        product = jnp.concatenate([src_re * rel_re - src_im * rel_im, src_re * rel_im + src_im * rel_re], axis=-1)
        positive = lax.optimization_barrier(jnp.sum(product * target, axis=-1))
        product_b = product.astype(jnp.bfloat16).astype(jnp.float32)
        negative = jnp.einsum('dek,dnk->den', product_b, negatives, precision=highest)
        grad_pos = -jax.nn.sigmoid(-positive)
        grad_neg = (neg_weight * jax.nn.sigmoid(negative)).astype(jnp.bfloat16).astype(jnp.float32)
        grad_q = grad_pos[..., None] * target + jnp.einsum('den,dnk->dek', grad_neg, negatives, precision=highest)
        grad_re, grad_im = (grad_q[..., :half_dim], grad_q[..., half_dim:])
        grad_src = jnp.concatenate([grad_re * rel_re + grad_im * rel_im, -grad_re * rel_im + grad_im * rel_re], axis=-1).astype(jnp.bfloat16)
        grad_rel = jnp.concatenate([grad_re * src_re + grad_im * src_im, -grad_re * src_im + grad_im * src_re], axis=-1).astype(jnp.bfloat16)
        grad_dst = (grad_pos[..., None] * product).astype(jnp.bfloat16)
        grad_negrow = jnp.einsum('den,dek->dnk', grad_neg, product_b, precision=highest).astype(jnp.bfloat16)
        left_grad = jnp.zeros((ENT, DIM), jnp.float32).at[src_index.reshape(-1)].add(grad_src.reshape(-1, DIM).astype(jnp.float32))
        right_grad = jnp.zeros((ENT, DIM), jnp.float32).at[dst_index.reshape(-1)].add(grad_dst.reshape(-1, DIM).astype(jnp.float32))
        right_grad = right_grad.at[neg_index.reshape(-1)].add(grad_negrow.reshape(-1, DIM).astype(jnp.float32))
        relation_grad = jnp.zeros((REL, DIM), jnp.float32).at[rel_index.reshape(-1)].add(grad_rel.reshape(-1, DIM).astype(jnp.float32))
        left_table, left_state = adagrad(left_table, left_state, left_grad)
        right_table, right_state = adagrad(right_table, right_state, right_grad)
        relations, relation_state = adagrad(relations, relation_state, relation_grad)
    return (left_table, left_state, right_table, right_state, relations, relation_state)
```

```python
import functools

import jax
import jax.numpy as jnp
from jax import lax
from jax.experimental import pallas as pl
from jax.experimental.pallas import tpu as pltpu
from jax.sharding import PartitionSpec as P

STEPS = 2


learn_rate = 0.1
neg_weight = 0.0625


def passed_along(value, axis, steps):
    count = lax.axis_size(axis)
    pairs = [(source, (source + steps) % count) for source in range(count)]
    return lax.ppermute(value, axis, pairs)


def adagrad(table, state, grad):
    state = state + jnp.mean(grad * grad, axis=-1)
    return (table - learn_rate * grad / jnp.sqrt(state)[:, None], state)


def spread_rows(matches, values):
    return lax.dot_general(
        matches, values, (((0,), (0,)), ((), ())), preferred_element_type=jnp.float32
    )


def lookup_fold(row_index, portion):
    portion_len = portion.shape[0]
    matches = (row_index[:, None] == jnp.arange(portion_len, dtype=jnp.int32)[None, :]).astype(
        jnp.bfloat16
    )
    return jnp.dot(matches, portion, preferred_element_type=jnp.float32)


def scatter_term(row_index, values, count):
    matches = (row_index[:, None] == jnp.arange(count, dtype=jnp.int32)[None, :]).astype(
        jnp.bfloat16
    )
    return spread_rows(matches, values)


MESH = pl.DeviceIdType.MESH


def remote(source, target, send_sem, recv_sem, device):
    return pltpu.make_async_remote_copy(
        src_ref=source,
        dst_ref=target,
        send_sem=send_sem,
        recv_sem=recv_sem,
        device_id=device,
        device_id_type=MESH,
    )


def sum_kernel(n_dom, grad_ref, out_ref, mine, other, half, parts, full, send_sems, recv_sems):
    group = 2 * n_dom
    rows = grad_ref.shape[0]
    half_rows = rows // 2
    piece = half_rows // group
    p = lax.axis_index("dom")
    e = lax.axis_index("edge")
    core = lax.rem(e, 2)
    me = p * 2 + e // 2
    sibling = (p, e + 1 - 2 * core)

    def peer(k):
        g = lax.rem(me + k, group)
        return (g // 2, lax.rem(g, 2) * 2 + core)

    barrier = pltpu.get_barrier_semaphore()
    pl.semaphore_signal(barrier, inc=1, device_id=sibling, device_id_type=MESH)

    def greet(k, carry):
        pl.semaphore_signal(barrier, inc=1, device_id=peer(k), device_id_type=MESH)
        return carry

    lax.fori_loop(1, group, greet, 0)
    theirs = pl.multiple_of((1 - core) * half_rows, half_rows)
    ours = pl.multiple_of(core * half_rows, half_rows)
    mine[...] = grad_ref[pl.ds(theirs, half_rows), :].astype(jnp.bfloat16)
    pl.semaphore_wait(barrier, group)
    swap = remote(mine, other, send_sems.at[0], recv_sems.at[0], sibling)
    swap.start()
    swap.wait()
    half[...] = (
        grad_ref[pl.ds(ours, half_rows), :] + other[...].astype(jnp.float32)
    ).astype(jnp.bfloat16)

    def spread(k, carry):
        g = lax.rem(me + k, group)
        start = pl.multiple_of(g * piece, piece)
        slot = pl.multiple_of((k - 1) * piece, piece)
        remote(
            half.at[pl.ds(start, piece)],
            parts.at[pl.ds(slot, piece)],
            send_sems.at[1],
            recv_sems.at[1],
            peer(k),
        ).start()
        return carry

    lax.fori_loop(1, group, spread, 0)
    many = pl.ds(0, (group - 1) * piece)
    pltpu.make_async_copy(parts.at[many], parts.at[many], recv_sems.at[1]).wait()
    own = pl.multiple_of(me * piece, piece)
    total = half[pl.ds(own, piece), :].astype(jnp.float32)
    for k in range(group - 1):
        total = total + parts[k * piece : (k + 1) * piece, :].astype(jnp.float32)
    place = pl.multiple_of(ours + own, piece)
    full[pl.ds(place, piece), :] = total.astype(jnp.bfloat16)
    pltpu.make_async_copy(parts.at[many], parts.at[many], send_sems.at[1]).wait()

    def gather(k, carry):
        remote(
            full.at[pl.ds(place, piece)],
            full.at[pl.ds(place, piece)],
            send_sems.at[2],
            recv_sems.at[2],
            peer(k),
        ).start()
        return carry

    lax.fori_loop(1, group, gather, 0)
    pltpu.make_async_copy(parts.at[many], parts.at[many], recv_sems.at[2]).wait()
    swap_back = remote(
        full.at[pl.ds(ours, half_rows)],
        full.at[pl.ds(ours, half_rows)],
        send_sems.at[3],
        recv_sems.at[3],
        sibling,
    )
    swap_back.start()
    pltpu.make_async_copy(parts.at[many], parts.at[many], send_sems.at[2]).wait()
    swap_back.wait()
    out_ref[...] = full[...].astype(jnp.float32)


def summed(grad, collective_id):
    rows, width = grad.shape
    half_rows = rows // 2
    return pl.pallas_call(
        functools.partial(sum_kernel, lax.axis_size("dom")),
        out_shape=jax.ShapeDtypeStruct(grad.shape, jnp.float32),
        in_specs=[pl.BlockSpec(memory_space=pltpu.VMEM)],
        out_specs=pl.BlockSpec(memory_space=pltpu.VMEM),
        scratch_shapes=[
            pltpu.VMEM((half_rows, width), jnp.bfloat16),
            pltpu.VMEM((half_rows, width), jnp.bfloat16),
            pltpu.VMEM((half_rows, width), jnp.bfloat16),
            pltpu.VMEM((half_rows, width), jnp.bfloat16),
            pltpu.VMEM((rows, width), jnp.bfloat16),
            pltpu.SemaphoreType.DMA((4,)),
            pltpu.SemaphoreType.DMA((4,)),
        ],
        name=f"relation_sum_{collective_id}",
        compiler_params=pltpu.CompilerParams(
            collective_id=collective_id, has_side_effects=True, vmem_limit_bytes=32 << 20
        ),
    )(grad)


def local(
    left_table,
    left_state,
    right_table,
    right_state,
    relations,
    relation_state,
    src_rows,
    dst_rows,
    rel_ids,
    neg_rows,
):
    quarter = left_table.shape[0]
    width = left_table.shape[1]
    half_dim = width // 2
    edge_count = src_rows.shape[1]
    rel_count = relations.shape[0]
    for bucket in range(STEPS):
        right_table, right_state = passed_along((right_table, right_state), "dom", 1)
        src_index = src_rows[bucket]
        target_index = jnp.concatenate([dst_rows[bucket], neg_rows[bucket]], axis=0)
        left_b = left_table.astype(jnp.bfloat16)
        right_b = right_table.astype(jnp.bfloat16)
        source = lookup_fold(src_index, lax.all_gather(left_b, "edge", axis=0, tiled=True))
        looked = lookup_fold(target_index, lax.all_gather(right_b, "edge", axis=0, tiled=True))
        target = looked[:edge_count]
        negatives_b = looked[edge_count:].astype(jnp.bfloat16)
        rel_matches = (
            rel_ids[bucket][:, None] == jnp.arange(rel_count, dtype=jnp.int32)[None, :]
        ).astype(jnp.bfloat16)
        relation = jnp.dot(
            rel_matches, relations.astype(jnp.bfloat16), preferred_element_type=jnp.float32
        )
        src_re, src_im = (source[:, :half_dim], source[:, half_dim:])
        rel_re, rel_im = (relation[:, :half_dim], relation[:, half_dim:])
        product = jnp.concatenate(
            [src_re * rel_re - src_im * rel_im, src_re * rel_im + src_im * rel_re], axis=-1
        )
        positive = jnp.sum(product * target, axis=-1)
        product_b = product.astype(jnp.bfloat16)
        negative = lax.dot_general(
            product_b, negatives_b, (((1,), (1,)), ((), ())), preferred_element_type=jnp.float32
        )
        grad_pos = -jax.nn.sigmoid(-positive)
        grad_neg = (neg_weight * jax.nn.sigmoid(negative)).astype(jnp.bfloat16)
        grad_q = grad_pos[:, None] * target + jnp.dot(
            grad_neg, negatives_b, preferred_element_type=jnp.float32
        )
        grad_re, grad_im = (grad_q[:, :half_dim], grad_q[:, half_dim:])
        grad_src = jnp.concatenate(
            [grad_re * rel_re + grad_im * rel_im, -grad_re * rel_im + grad_im * rel_re], axis=-1
        ).astype(jnp.bfloat16)
        grad_rel = jnp.concatenate(
            [grad_re * src_re + grad_im * src_im, -grad_re * src_im + grad_im * src_re], axis=-1
        ).astype(jnp.bfloat16)
        grad_dst = (grad_pos[:, None] * product).astype(jnp.bfloat16)
        grad_negrow = spread_rows(grad_neg, product_b).astype(jnp.bfloat16)
        grad_target = jnp.concatenate([grad_dst, grad_negrow], axis=0)
        left_grad = lax.psum_scatter(
            scatter_term(src_index, grad_src, quarter * lax.axis_size("edge")),
            "edge",
            scatter_dimension=0,
            tiled=True,
        )
        right_grad = lax.psum_scatter(
            scatter_term(target_index, grad_target, quarter * lax.axis_size("edge")),
            "edge",
            scatter_dimension=0,
            tiled=True,
        )
        relation_grad = summed(spread_rows(rel_matches, grad_rel), bucket)
        left_table, left_state = adagrad(left_table, left_state, left_grad)
        right_table, right_state = adagrad(right_table, right_state, right_grad)
        relations, relation_state = adagrad(relations, relation_state, relation_grad)
    return (left_table, left_state, right_table, right_state, relations, relation_state)


def solution(mesh):
    placed = (
        P(("dom", "edge"), None),
        P(("dom", "edge")),
        P(("dom", "edge"), None),
        P(("dom", "edge")),
        P(),
        P(),
        P(None, ("dom", "edge")),
        P(None, ("dom", "edge")),
        P(None, ("dom", "edge")),
        P(None, ("dom", "edge")),
    )
    return jax.shard_map(
        local,
        mesh=mesh,
        in_specs=placed,
        out_specs=(
            P(("dom", "edge"), None),
            P(("dom", "edge")),
            P(("dom", "edge"), None),
            P(("dom", "edge")),
            P(),
            P(),
        ),
        check_vma=False,
    )
```

```python
import functools

import jax
import jax.numpy as jnp
from jax import lax
from jax.experimental import pallas as pl
from jax.experimental.pallas import tpu as pltpu
from jax.sharding import PartitionSpec as P

STEPS = 2
LANES = 128
CHUNK = 256
ROLL_PARTS = 2
MESH = pl.DeviceIdType.MESH
learn_rate = 0.1
neg_weight = 0.0625


def eye(kind=jnp.float32):
    rows = lax.broadcasted_iota(jnp.int32, (LANES, LANES), 0)
    columns = lax.broadcasted_iota(jnp.int32, (LANES, LANES), 1)
    return rows == columns


def to_column(row):
    spread = jnp.where(eye(), jnp.broadcast_to(row, (LANES, LANES)), 0.0)
    return jnp.sum(spread, axis=1, keepdims=True)


def to_row(column):
    spread = jnp.where(eye(), jnp.broadcast_to(column, (LANES, LANES)), 0.0)
    return jnp.sum(spread, axis=0, keepdims=True)


def body(
    n_dom,
    left_in,
    left_state_in,
    right_in,
    right_state_in,
    rel_in,
    rel_state_in,
    src_in,
    dst_in,
    rel_ids_in,
    neg_in,
    left_out,
    left_state_out,
    right_out,
    right_state_out,
    rel_out,
    rel_state_out,
    high_col,
    low_col,
    high_row,
    low_row,
    rel_b,
    source,
    target,
    relation,
    negatives,
    product_b,
    grad_src,
    grad_rel,
    grad_target,
    grad_neg_acc,
    left_all,
    right_all,
    right_own,
    right_table,
    right_state,
    right_next,
    right_state_next,
    left_far_sum,
    left_own_sum,
    right_far_sum,
    right_own_sum,
    rel_own_sum,
    left_to_sib,
    left_from_sib,
    left_to_far,
    left_from_far,
    right_to_sib,
    right_from_sib,
    right_to_far,
    right_from_far,
    rel_to_sib,
    rel_from_sib,
    rel_half,
    rel_parts,
    rel_full,
    send_sems,
    recv_sems,
):
    f32, bf16 = jnp.float32, jnp.bfloat16
    quarter, width = left_in.shape
    edges = src_in.shape[1]
    negs = neg_in.shape[1]
    rels = rel_in.shape[0]
    half_dim = width // 2
    blocks = quarter // LANES
    group = 2 * n_dom
    half_rows = rels // 2
    piece = half_rows // group
    src_at, rel_at, target_at = 0, edges, 2 * edges
    targets = edges + negs

    p = lax.axis_index("dom")
    e = lax.axis_index("edge")
    core = lax.rem(e, 2)
    side = e // 2
    me = p * 2 + side
    sibling = (p, side * 2 + 1 - core)
    far = (p, (1 - side) * 2 + core)
    following = (lax.rem(p + 1, n_dom), e)
    near_quarter = side * 2 + core
    sib_quarter = side * 2 + 1 - core
    far_quarter = (1 - side) * 2 + core
    far_sib_quarter = (1 - side) * 2 + 1 - core

    def peer(k):
        g = lax.rem(me + k, group)
        return (g // 2, lax.rem(g, 2) * 2 + core)

    def rows_of(index, size=quarter):
        return pl.ds(pl.multiple_of(index * size, size), size)

    used = [0]
    sent = []

    def copy(source_ref, target_ref, device):
        index = used[0]
        used[0] += 1
        made = pltpu.make_async_remote_copy(
            src_ref=source_ref,
            dst_ref=target_ref,
            send_sem=send_sems.at[index],
            recv_sem=recv_sems.at[index],
            device_id=device,
            device_id_type=MESH,
        )
        made.start()
        sent.append(made)
        return made

    def each(count, step):
        def run(i, carry):
            step(i)
            return carry

        lax.fori_loop(0, count, run, 0)

    def prepare(t):
        lists = (
            (src_in, src_at, edges),
            (rel_ids_in, rel_at, edges),
            (dst_in, target_at, edges),
            (neg_in, target_at + edges, negs),
        )
        for ref, at, count in lists:

            def block(j, ref=ref, at=at):
                row = ref[t : t + 1, pl.ds(pl.multiple_of(j * LANES, LANES), LANES)]
                place = pl.ds(pl.multiple_of(at + j * LANES, LANES), LANES)
                high = (row >> 7).astype(f32)
                low = (row & 127).astype(f32)
                lanes = lax.broadcasted_iota(jnp.int32, (LANES, LANES), 1).astype(f32)
                subs = lax.broadcasted_iota(jnp.int32, (LANES, LANES), 0).astype(f32)
                low_row[t, :, place] = jnp.where(subs == low, 1.0, 0.0).astype(bf16)
                high_row[t, :, place] = jnp.broadcast_to(high, (16, LANES)).astype(bf16)
                column = jnp.broadcast_to(to_column(row.astype(f32)), (LANES, LANES))
                high_c = jnp.floor(column * (1.0 / LANES))
                low_c = column - LANES * high_c
                high_col[t, place, :] = high_c.astype(bf16)
                low_col[t, place, :] = jnp.where(lanes == low_c, 1.0, 0.0).astype(bf16)

            each(count // LANES, block)

    def level(index, shape):
        return jnp.full(shape, jnp.asarray(index, jnp.int32).astype(f32), f32).astype(bf16)

    def lookup(t, at, count, first_block, n_blocks, table, out, fresh):
        def chunk(i):
            place = pl.ds(pl.multiple_of(at + i * CHUNK, CHUNK), CHUNK)
            high = high_col[t, place, :]
            low = low_col[t, place, :]
            zero = jnp.zeros_like(low)
            matches = jnp.concatenate(
                [
                    jnp.where(high == level(first_block + j, high.shape), low, zero)
                    for j in range(n_blocks)
                ],
                axis=1,
            )
            found = jnp.dot(matches, table[...], preferred_element_type=f32)
            dest = pl.ds(pl.multiple_of(i * CHUNK, CHUNK), CHUNK)
            if fresh:
                out[dest, :] = found
            else:
                out[dest, :] += found

        each(count // CHUNK, chunk)

    def scatter(t, at, count, first_block, n_blocks, values, store):
        def pair(i):
            high = high_row[t, :, at : at + count]
            low = low_row[t, :, at : at + count]
            one, none = jnp.ones_like(high), jnp.zeros_like(high)
            parts = []
            for j in range(2):
                hit = jnp.where(high == level(first_block + 2 * i + j, high.shape), one, none)
                parts.append(low * jnp.concatenate([hit] * (LANES // 16), axis=0))
            matches = jnp.concatenate(parts, axis=0)
            store(
                pl.ds(pl.multiple_of(i * 2 * LANES, 2 * LANES), 2 * LANES),
                jnp.dot(matches, values[...], preferred_element_type=f32),
            )

        each(n_blocks // 2, pair)

    def dense(t):
        negatives[...] = target[edges:, :].astype(bf16)
        grad_neg_acc[...] = jnp.zeros_like(grad_neg_acc)

        def chunk(i):
            place = pl.ds(pl.multiple_of(i * CHUNK, CHUNK), CHUNK)
            s_re, s_im = source[place, :half_dim], source[place, half_dim:]
            r_re, r_im = relation[place, :half_dim], relation[place, half_dim:]
            goal = target[place, :]
            product = jnp.concatenate(
                [s_re * r_re - s_im * r_im, s_re * r_im + s_im * r_re], axis=1
            )
            positive = jnp.sum(product * goal, axis=1, keepdims=True)
            rounded = product.astype(bf16)
            product_b[place, :] = rounded
            n_b = negatives[...]
            negative = lax.dot_general(
                rounded, n_b, (((1,), (1,)), ((), ())), preferred_element_type=f32
            )
            g_pos = -1.0 / (1.0 + jnp.exp(positive))
            g_neg = (neg_weight / (1.0 + jnp.exp(-negative))).astype(bf16)
            g_q = g_pos * goal + jnp.dot(g_neg, n_b, preferred_element_type=f32)
            g_re, g_im = g_q[:, :half_dim], g_q[:, half_dim:]
            grad_src[place, :half_dim] = (g_re * r_re + g_im * r_im).astype(bf16)
            grad_src[place, half_dim:] = (g_im * r_re - g_re * r_im).astype(bf16)
            grad_rel[place, :half_dim] = (g_re * s_re + g_im * s_im).astype(bf16)
            grad_rel[place, half_dim:] = (g_im * s_re - g_re * s_im).astype(bf16)
            grad_target[place, :] = (g_pos * product).astype(bf16)
            grad_neg_acc[...] += lax.dot_general(
                g_neg, rounded, (((0,), (0,)), ((), ())), preferred_element_type=f32
            )

        each(edges // CHUNK, chunk)
        grad_target[edges:, :] = grad_neg_acc[...].astype(bf16)

    def adagrad(table, state, grad_of, table_to, state_to, block):
        place = rows_of(block, LANES)
        grad = grad_of(place)
        column = to_column(state[pl.ds(block, 1), :])
        column = column + jnp.mean(grad * grad, axis=1, keepdims=True)
        table_to[place, :] = table[place, :] - learn_rate * grad / jnp.sqrt(column)
        state_to[pl.ds(block, 1), :] = to_row(column)

    def reduce_begin(t, at, count, values, to_sib, from_sib, far_sum, own_sum):
        copies = []
        for i, quarter_index in enumerate((far_sib_quarter, sib_quarter)):

            def store(place, value, i=i):
                to_sib[t, i, place, :] = value.astype(bf16)

            scatter(t, at, count, quarter_index * blocks, blocks, values, store)
            copies.append(copy(to_sib.at[t, i], from_sib.at[t, i], sibling))
        for quarter_index, total in ((far_quarter, far_sum), (near_quarter, own_sum)):

            def keep(place, value, total=total):
                total[place, :] = value

            scatter(t, at, count, quarter_index * blocks, blocks, values, keep)
        return copies

    def reduce_far(t, copies, from_sib, far_sum, to_far, from_far):
        copies[0].wait_recv()
        to_far[t] = (far_sum[...] + from_sib[t, 0].astype(f32)).astype(bf16)
        return copy(to_far.at[t], from_far.at[t], far)

    def reduce_end(t, copies, far_copy, own_sum, from_sib, from_far):
        copies[1].wait_recv()
        far_copy.wait_recv()

        def grad_of(place):
            return (
                own_sum[place, :]
                + from_sib[t, 1, place, :].astype(f32)
                + from_far[t, place, :].astype(f32)
            )

        return grad_of

    def rel_begin(t):
        pairs = half_rows // LANES

        def store(place, value):
            rel_to_sib[t, place, :] = value.astype(bf16)

        scatter(t, rel_at, edges, (1 - core) * pairs, pairs, grad_rel, store)
        swap = copy(rel_to_sib.at[t], rel_from_sib.at[t], sibling)

        def keep(place, value):
            rel_own_sum[place, :] = value

        scatter(t, rel_at, edges, core * pairs, pairs, grad_rel, keep)
        return swap

    many = pl.ds(0, (group - 1) * piece)

    def take_sems():
        index = used[0]
        used[0] += 1
        return send_sems.at[index], recv_sems.at[index]

    def wait_many(t, sem):
        whole = rel_parts.at[t, many]
        pltpu.make_async_copy(whole, whole, sem).wait()

    def rel_spread(t, swap):
        swap.wait_recv()
        rel_half[t] = (rel_own_sum[...] + rel_from_sib[t].astype(f32)).astype(bf16)
        sems = take_sems()

        def send(k):
            k = k + 1
            g = lax.rem(me + k, group)
            pltpu.make_async_remote_copy(
                src_ref=rel_half.at[t, rows_of(g, piece)],
                dst_ref=rel_parts.at[t, rows_of(k - 1, piece)],
                send_sem=sems[0],
                recv_sem=sems[1],
                device_id=peer(k),
                device_id_type=MESH,
            ).start()

        each(group - 1, send)
        return sems

    def rel_gather(t, sems):
        wait_many(t, sems[1])
        total = rel_half[t, rows_of(me, piece), :].astype(f32)
        for k in range(group - 1):
            total = total + rel_parts[t, k * piece : (k + 1) * piece, :].astype(f32)
        place = rows_of(core * group + me, piece)
        rel_full[t, place, :] = total.astype(bf16)
        more = take_sems()

        def send(k):
            pltpu.make_async_remote_copy(
                src_ref=rel_full.at[t, place],
                dst_ref=rel_full.at[t, place],
                send_sem=more[0],
                recv_sem=more[1],
                device_id=peer(k + 1),
                device_id_type=MESH,
            ).start()

        each(group - 1, send)
        wait_many(t, sems[0])
        return more

    def rel_back(t, more):
        wait_many(t, more[1])
        ours = rows_of(core, half_rows)
        back = copy(rel_full.at[t, ours], rel_full.at[t, ours], sibling)
        wait_many(t, more[0])
        return back

    def rel_update(t, back, table, state):
        back.wait_recv()

        def block(i):
            def grad_of(place):
                return rel_full[t, place, :].astype(f32)

            adagrad(table, state, grad_of, rel_out, rel_state_out, i)

        each(rels // LANES, block)

    def round_relations(table):
        def block(i):
            place = rows_of(i, CHUNK)
            rel_b[place, :] = table[place, :].astype(bf16)

        each(rels // CHUNK, block)

    def left_send(t):
        mine = left_all.at[t, rows_of(near_quarter)]
        return copy(mine, mine, far), copy(mine, mine, sibling)

    def left_forward(t, far_copy):
        far_copy.wait_recv()
        theirs = left_all.at[t, rows_of(far_quarter)]
        return copy(theirs, theirs, sibling)

    part = quarter // ROLL_PARTS

    def part_of(index, i):
        return pl.ds(pl.multiple_of(index * quarter + i * part, part), part)

    def right_send(t):
        return [
            copy(
                right_own.at[t, pl.ds(i * part, part)],
                right_all.at[t, part_of(near_quarter, i)],
                following,
            )
            for i in range(ROLL_PARTS)
        ]

    def right_spread(t, rolled):
        to_far, to_sib = [], []
        for i, made in enumerate(rolled):
            made.wait_recv()
            mine = right_all.at[t, part_of(near_quarter, i)]
            to_far.append(copy(mine, mine, far))
            to_sib.append(copy(mine, mine, sibling))
        return to_far, to_sib

    def right_forward(t, to_far):
        forwarded = []
        for i, made in enumerate(to_far):
            made.wait_recv()
            theirs = right_all.at[t, part_of(far_quarter, i)]
            forwarded.append(copy(theirs, theirs, sibling))
        return forwarded

    def wait_all(copies):
        for made in copies:
            made.wait_recv()

    def look_left(t, index, fresh=False):
        lookup(
            t, src_at, edges, index * blocks, blocks, left_all.at[t, rows_of(index)], source, fresh
        )

    def look_right(t, index, fresh=False):
        lookup(
            t,
            target_at,
            targets,
            index * blocks,
            blocks,
            right_all.at[t, rows_of(index)],
            target,
            fresh,
        )

    def look_relation(t):
        lookup(t, rel_at, edges, 0, rels // LANES, rel_b, relation, True)

    def update(table, state, grad_of, table_to, state_to):
        each(blocks, functools.partial(adagrad, table, state, grad_of, table_to, state_to))

    barrier = pltpu.get_barrier_semaphore()
    pl.semaphore_signal(barrier, inc=1, device_id=sibling, device_id_type=MESH)

    def greet(k):
        pl.semaphore_signal(barrier, inc=1, device_id=peer(k + 1), device_id_type=MESH)

    each(group - 1, greet)
    left_all[0, rows_of(near_quarter), :] = left_in[...].astype(bf16)
    right_own[0] = right_in[...].astype(bf16)
    pl.semaphore_wait(barrier, group)

    rolled = right_send(0)
    left_far, left_sib = left_send(0)
    round_relations(rel_in)
    prepare(0)
    look_relation(0)
    look_left(0, near_quarter, True)
    left_sib.wait_recv()
    look_left(0, sib_quarter)
    right_far, right_sib = right_spread(0, rolled)
    table_roll = copy(right_in, right_table.at[0], following)
    state_roll = copy(right_state_in, right_state.at[0], following)
    left_far_sib = left_forward(0, left_far)
    look_left(0, far_quarter)
    look_right(0, near_quarter, True)
    left_far_sib.wait_recv()
    look_left(0, far_sib_quarter)
    wait_all(right_sib)
    look_right(0, sib_quarter)
    prepare(1)
    right_far_sib = right_forward(0, right_far)
    look_right(0, far_quarter)
    wait_all(right_far_sib)
    look_right(0, far_sib_quarter)
    dense(0)

    right_copies = reduce_begin(
        0, target_at, targets, grad_target, right_to_sib, right_from_sib, right_far_sum, right_own_sum
    )
    right_home = reduce_far(0, right_copies, right_from_sib, right_far_sum, right_to_far, right_from_far)
    swap = rel_begin(0)
    spread = rel_spread(0, swap)
    left_copies = reduce_begin(
        0, src_at, edges, grad_src, left_to_sib, left_from_sib, left_far_sum, left_own_sum
    )
    left_home = reduce_far(0, left_copies, left_from_sib, left_far_sum, left_to_far, left_from_far)
    table_roll.wait_recv()
    state_roll.wait_recv()
    right_grad = reduce_end(0, right_copies, right_home, right_own_sum, right_from_sib, right_from_far)
    update(right_table.at[0], right_state.at[0], right_grad, right_next, right_state_next)
    right_own[1] = right_next[...].astype(bf16)
    rolled = right_send(1)
    gathered = rel_gather(0, spread)
    left_grad = reduce_end(0, left_copies, left_home, left_own_sum, left_from_sib, left_from_far)
    update(left_in, left_state_in, left_grad, left_out, left_state_out)
    left_all[1, rows_of(near_quarter), :] = left_out[...].astype(bf16)
    left_far, left_sib = left_send(1)
    right_far, right_sib = right_spread(1, rolled)
    table_roll = copy(right_next, right_table.at[1], following)
    state_roll = copy(right_state_next, right_state.at[1], following)
    back = rel_back(0, gathered)
    look_left(1, near_quarter, True)
    left_sib.wait_recv()
    look_left(1, sib_quarter)
    left_far_sib = left_forward(1, left_far)
    rel_update(0, back, rel_in, rel_state_in)
    round_relations(rel_out)
    look_relation(1)
    look_left(1, far_quarter)
    left_far_sib.wait_recv()
    look_left(1, far_sib_quarter)
    look_right(1, near_quarter, True)
    wait_all(right_sib)
    look_right(1, sib_quarter)
    right_far_sib = right_forward(1, right_far)
    look_right(1, far_quarter)
    wait_all(right_far_sib)
    look_right(1, far_sib_quarter)
    dense(1)

    swap = rel_begin(1)
    spread = rel_spread(1, swap)
    right_copies = reduce_begin(
        1, target_at, targets, grad_target, right_to_sib, right_from_sib, right_far_sum, right_own_sum
    )
    right_home = reduce_far(1, right_copies, right_from_sib, right_far_sum, right_to_far, right_from_far)
    left_copies = reduce_begin(
        1, src_at, edges, grad_src, left_to_sib, left_from_sib, left_far_sum, left_own_sum
    )
    left_home = reduce_far(1, left_copies, left_from_sib, left_far_sum, left_to_far, left_from_far)
    gathered = rel_gather(1, spread)
    table_roll.wait_recv()
    state_roll.wait_recv()
    right_grad = reduce_end(1, right_copies, right_home, right_own_sum, right_from_sib, right_from_far)
    update(right_table.at[1], right_state.at[1], right_grad, right_out, right_state_out)
    left_grad = reduce_end(1, left_copies, left_home, left_own_sum, left_from_sib, left_from_far)
    update(left_out, left_state_out, left_grad, left_out, left_state_out)
    back = rel_back(1, gathered)
    rel_update(1, back, rel_out, rel_state_out)
    for made in sent:
        made.wait_send()


def local(
    left_table,
    left_state,
    right_table,
    right_state,
    relations,
    relation_state,
    src_rows,
    dst_rows,
    rel_ids,
    neg_rows,
):
    quarter, width = left_table.shape
    edges = src_rows.shape[1]
    negs = neg_rows.shape[1]
    rels = relations.shape[0]
    slab = quarter * lax.axis_size("edge")
    indices = 3 * edges + negs
    targets = edges + negs
    f32, bf16 = jnp.float32, jnp.bfloat16
    state_shape = (quarter // LANES, LANES)
    rel_state_shape = (rels // LANES, LANES)

    def vmem(shape, kind):
        return pltpu.VMEM(shape, kind)

    results = pl.pallas_call(
        functools.partial(body, lax.axis_size("dom")),
        out_shape=(
            jax.ShapeDtypeStruct((quarter, width), f32),
            jax.ShapeDtypeStruct(state_shape, f32),
            jax.ShapeDtypeStruct((quarter, width), f32),
            jax.ShapeDtypeStruct(state_shape, f32),
            jax.ShapeDtypeStruct((rels, width), f32),
            jax.ShapeDtypeStruct(rel_state_shape, f32),
        ),
        in_specs=[pl.BlockSpec(memory_space=pltpu.VMEM)] * 10,
        out_specs=tuple([pl.BlockSpec(memory_space=pltpu.VMEM)] * 6),
        scratch_shapes=[
            vmem((STEPS, indices, LANES), bf16),
            vmem((STEPS, indices, LANES), bf16),
            vmem((STEPS, 16, indices), bf16),
            vmem((STEPS, LANES, indices), bf16),
            vmem((rels, width), bf16),
            vmem((edges, width), f32),
            vmem((targets, width), f32),
            vmem((edges, width), f32),
            vmem((negs, width), bf16),
            vmem((edges, width), bf16),
            vmem((edges, width), bf16),
            vmem((edges, width), bf16),
            vmem((targets, width), bf16),
            vmem((negs, width), f32),
            vmem((STEPS, slab, width), bf16),
            vmem((STEPS, slab, width), bf16),
            vmem((STEPS, quarter, width), bf16),
            vmem((STEPS, quarter, width), f32),
            vmem((STEPS,) + state_shape, f32),
            vmem((quarter, width), f32),
            vmem(state_shape, f32),
            vmem((quarter, width), f32),
            vmem((quarter, width), f32),
            vmem((quarter, width), f32),
            vmem((quarter, width), f32),
            vmem((rels // 2, width), f32),
            vmem((STEPS, 2, quarter, width), bf16),
            vmem((STEPS, 2, quarter, width), bf16),
            vmem((STEPS, quarter, width), bf16),
            vmem((STEPS, quarter, width), bf16),
            vmem((STEPS, 2, quarter, width), bf16),
            vmem((STEPS, 2, quarter, width), bf16),
            vmem((STEPS, quarter, width), bf16),
            vmem((STEPS, quarter, width), bf16),
            vmem((STEPS, rels // 2, width), bf16),
            vmem((STEPS, rels // 2, width), bf16),
            vmem((STEPS, rels // 2, width), bf16),
            vmem((STEPS, rels // 2, width), bf16),
            vmem((STEPS, rels, width), bf16),
            pltpu.SemaphoreType.DMA((64,)),
            pltpu.SemaphoreType.DMA((64,)),
        ],
        name="buckets",
        compiler_params=pltpu.CompilerParams(
            collective_id=0, has_side_effects=True, vmem_limit_bytes=56 << 20
        ),
    )(
        left_table,
        left_state.reshape(state_shape),
        right_table,
        right_state.reshape(state_shape),
        relations,
        relation_state.reshape(rel_state_shape),
        src_rows,
        dst_rows,
        rel_ids,
        neg_rows,
    )
    left, left_s, right, right_s, rel, rel_s = results
    return (left, left_s.reshape(-1), right, right_s.reshape(-1), rel, rel_s.reshape(-1))


def solution(mesh):
    placed = (
        P(("dom", "edge"), None),
        P(("dom", "edge")),
        P(("dom", "edge"), None),
        P(("dom", "edge")),
        P(),
        P(),
        P(None, ("dom", "edge")),
        P(None, ("dom", "edge")),
        P(None, ("dom", "edge")),
        P(None, ("dom", "edge")),
    )
    return jax.shard_map(
        local,
        mesh=mesh,
        in_specs=placed,
        out_specs=(
            P(("dom", "edge"), None),
            P(("dom", "edge")),
            P(("dom", "edge"), None),
            P(("dom", "edge")),
            P(),
            P(),
        ),
        check_vma=False,
    )
```

```python
import functools

import jax
import jax.numpy as jnp
from jax import lax
from jax.experimental import pallas as pl
from jax.experimental.pallas import tpu as pltpu
from jax.sharding import PartitionSpec as P

STEPS = 2
LANES = 128
CHUNK = 256
ROLL_PARTS = 2
FINISH = 4
MESH = pl.DeviceIdType.MESH
learn_rate = 0.1
neg_weight = 0.0625


def eye(kind=jnp.float32):
    rows = lax.broadcasted_iota(jnp.int32, (LANES, LANES), 0)
    columns = lax.broadcasted_iota(jnp.int32, (LANES, LANES), 1)
    return rows == columns


def to_column(row):
    spread = jnp.where(eye(), jnp.broadcast_to(row, (LANES, LANES)), 0.0)
    return jnp.sum(spread, axis=1, keepdims=True)


def to_row(column):
    spread = jnp.where(eye(), jnp.broadcast_to(column, (LANES, LANES)), 0.0)
    return jnp.sum(spread, axis=0, keepdims=True)


def adagrad(table, state, grad):
    column = to_column(state) + jnp.mean(grad * grad, axis=1, keepdims=True)
    return table - learn_rate * grad / jnp.sqrt(column), to_row(column)


def body(
    n_dom,
    left_in,
    left_state_in,
    right_in,
    right_state_in,
    rel_in,
    rel_state_in,
    src_in,
    dst_in,
    rel_ids_in,
    neg_in,
    left_out,
    left_state_out,
    right_out,
    right_state_out,
    rel_out,
    rel_state_out,
    rel_grad_out,
    left,
    right,
    rel,
    high_col,
    low_col,
    high_row,
    low_row,
    rel_b,
    source,
    target,
    relation,
    negatives,
    product_b,
    grad_src,
    grad_rel,
    grad_target,
    grad_neg_acc,
    left_all,
    right_all,
    right_own,
    right_low_own,
    right_low,
    right_state,
    right_state_next,
    left_far_sum,
    left_own_sum,
    right_far_sum,
    right_own_sum,
    rel_own_sum,
    left_to_sib,
    left_from_sib,
    left_to_far,
    left_from_far,
    right_to_sib,
    right_from_sib,
    right_to_far,
    right_from_far,
    rel_to_sib,
    rel_from_sib,
    rel_half,
    rel_parts,
    rel_line,
    rel_full,
    send_sems,
    recv_sems,
    local_sems,
):
    f32, bf16 = jnp.float32, jnp.bfloat16
    quarter, width = left_in.shape
    edges = src_in.shape[1]
    negs = neg_in.shape[1]
    rels = rel_in.shape[0]
    half_dim = width // 2
    blocks = quarter // LANES
    half_rows = rels // 2
    n_y = 4 if n_dom % 8 == 0 else 2
    n_low = 2
    n_z = n_dom // (n_y * n_low)
    plane = n_z * n_y
    line = 2 * n_low
    piece = half_rows // plane
    src_at, rel_at, target_at = 0, edges, 2 * edges
    targets = edges + negs

    p = lax.axis_index("dom")
    e = lax.axis_index("edge")
    core = lax.rem(e, 2)
    side = e // 2
    z, x_low, y = p // (n_y * n_low), lax.rem(p // n_y, n_low), lax.rem(p, n_y)
    at_plane = z * n_y + y
    at_line = side * n_low + x_low
    sibling = (p, side * 2 + 1 - core)
    far = (p, (1 - side) * 2 + core)
    following = (lax.rem(p + 1, n_dom), e)
    preceding = (lax.rem(p + n_dom - 1, n_dom), e)
    near_quarter = side * 2 + core
    sib_quarter = side * 2 + 1 - core
    far_quarter = (1 - side) * 2 + core
    far_sib_quarter = (1 - side) * 2 + 1 - core

    def plane_peer(k):
        g = lax.rem(at_plane + k, plane)
        return (g // n_y * (n_y * n_low) + x_low * n_y + lax.rem(g, n_y), e)

    def line_peer(k):
        g = lax.rem(at_line + k, line)
        return (z * (n_y * n_low) + lax.rem(g, n_low) * n_y + y, g // n_low * 2 + core)

    def rows_of(index, size=quarter):
        return pl.ds(pl.multiple_of(index * size, size), size)

    used = [0]
    sent = []

    def copy(source_ref, target_ref, device):
        index = used[0]
        used[0] += 1
        made = pltpu.make_async_remote_copy(
            src_ref=source_ref,
            dst_ref=target_ref,
            send_sem=send_sems.at[index],
            recv_sem=recv_sems.at[index],
            device_id=device,
            device_id_type=MESH,
        )
        made.start()
        sent.append(made)
        return made

    def each(count, step):
        def run(i, carry):
            step(i)
            return carry

        lax.fori_loop(0, count, run, 0)

    def prepare(t):
        lists = (
            (src_in, src_at, edges),
            (rel_ids_in, rel_at, edges),
            (dst_in, target_at, edges),
            (neg_in, target_at + edges, negs),
        )
        for ref, at, count in lists:

            def block(j, ref=ref, at=at):
                row = ref[t : t + 1, pl.ds(pl.multiple_of(j * LANES, LANES), LANES)]
                place = pl.ds(pl.multiple_of(at + j * LANES, LANES), LANES)
                high = (row >> 7).astype(f32)
                low = (row & 127).astype(f32)
                lanes = lax.broadcasted_iota(jnp.int32, (LANES, LANES), 1).astype(f32)
                subs = lax.broadcasted_iota(jnp.int32, (LANES, LANES), 0).astype(f32)
                low_row[t, :, place] = jnp.where(subs == low, 1.0, 0.0).astype(bf16)
                high_row[t, :, place] = jnp.broadcast_to(high, (16, LANES)).astype(bf16)
                column = jnp.broadcast_to(to_column(row.astype(f32)), (LANES, LANES))
                high_c = jnp.floor(column * (1.0 / LANES))
                low_c = column - LANES * high_c
                high_col[t, place, :] = high_c.astype(bf16)
                low_col[t, place, :] = jnp.where(lanes == low_c, 1.0, 0.0).astype(bf16)

            for j in range(count // LANES):
                block(j)

    def level(index, shape):
        return jnp.full(shape, jnp.asarray(index, jnp.int32).astype(f32), f32).astype(bf16)

    def lookup(t, at, count, first_block, n_blocks, table, out, fresh):
        def chunk(i):
            place = pl.ds(pl.multiple_of(at + i * CHUNK, CHUNK), CHUNK)
            high = high_col[t, place, :]
            low = low_col[t, place, :]
            zero = jnp.zeros_like(low)
            matches = jnp.concatenate(
                [
                    jnp.where(high == level(first_block + j, high.shape), low, zero)
                    for j in range(n_blocks)
                ],
                axis=1,
            )
            found = jnp.dot(matches, table[...], preferred_element_type=f32)
            dest = pl.ds(pl.multiple_of(i * CHUNK, CHUNK), CHUNK)
            if fresh:
                out[dest, :] = found
            else:
                out[dest, :] += found

        for i in range(count // CHUNK):
            chunk(i)

    def scatter(t, at, count, first_block, n_blocks, values, store):
        def pair(i):
            high = high_row[t, :, at : at + count]
            low = low_row[t, :, at : at + count]
            one, none = jnp.ones_like(high), jnp.zeros_like(high)
            parts = []
            for j in range(2):
                hit = jnp.where(high == level(first_block + 2 * i + j, high.shape), one, none)
                parts.append(low * jnp.concatenate([hit] * (LANES // 16), axis=0))
            matches = jnp.concatenate(parts, axis=0)
            store(
                pl.ds(pl.multiple_of(i * 2 * LANES, 2 * LANES), 2 * LANES),
                jnp.dot(matches, values[...], preferred_element_type=f32),
            )

        for i in range(n_blocks // 2):
            pair(i)

    def dense(t):
        negatives[...] = target[edges:, :].astype(bf16)
        grad_neg_acc[...] = jnp.zeros_like(grad_neg_acc)

        def chunk(i):
            place = pl.ds(pl.multiple_of(i * CHUNK, CHUNK), CHUNK)
            s_re, s_im = source[place, :half_dim], source[place, half_dim:]
            r_re, r_im = relation[place, :half_dim], relation[place, half_dim:]
            goal = target[place, :]
            product = jnp.concatenate(
                [s_re * r_re - s_im * r_im, s_re * r_im + s_im * r_re], axis=1
            )
            positive = jnp.sum(product * goal, axis=1, keepdims=True)
            rounded = product.astype(bf16)
            product_b[place, :] = rounded
            n_b = negatives[...]
            negative = lax.dot_general(
                rounded, n_b, (((1,), (1,)), ((), ())), preferred_element_type=f32
            )
            g_pos = -1.0 / (1.0 + jnp.exp(positive))
            g_neg = (neg_weight / (1.0 + jnp.exp(-negative))).astype(bf16)
            g_q = g_pos * goal + jnp.dot(g_neg, n_b, preferred_element_type=f32)
            g_re, g_im = g_q[:, :half_dim], g_q[:, half_dim:]
            grad_src[place, :half_dim] = (g_re * r_re + g_im * r_im).astype(bf16)
            grad_src[place, half_dim:] = (g_im * r_re - g_re * r_im).astype(bf16)
            grad_rel[place, :half_dim] = (g_re * s_re + g_im * s_im).astype(bf16)
            grad_rel[place, half_dim:] = (g_im * s_re - g_re * s_im).astype(bf16)
            grad_target[place, :] = (g_pos * product).astype(bf16)
            grad_neg_acc[...] += lax.dot_general(
                g_neg, rounded, (((0,), (0,)), ((), ())), preferred_element_type=f32
            )

        each(edges // CHUNK, chunk)
        grad_target[edges:, :] = grad_neg_acc[...].astype(bf16)

    def fetch(source_ref, target_ref, index):
        made = pltpu.make_async_copy(source_ref, target_ref, local_sems.at[index])
        made.start()
        return made

    def update(count, table_of, state, grad_of, store, state_to):
        for i in range(count // LANES):
            place = pl.ds(i * LANES, LANES)
            value, row = adagrad(table_of(place), state[i : i + 1, :], grad_of(place))
            store(place, value)
            state_to[i : i + 1, :] = row

    def reduce_begin(t, at, count, values, to_sib, from_sib, far_sum, own_sum, to_far, from_far):
        copies = []

        def give(i, quarter_index):
            def store(place, value):
                to_sib[t, i, place, :] = value.astype(bf16)

            scatter(t, at, count, quarter_index * blocks, blocks, values, store)
            copies.append(copy(to_sib.at[t, i], from_sib.at[t, i], sibling))

        def keep(quarter_index, total):
            def store(place, value):
                total[place, :] = value

            scatter(t, at, count, quarter_index * blocks, blocks, values, store)

        give(0, far_sib_quarter)
        keep(far_quarter, far_sum)
        copies[0].wait_recv()
        to_far[t] = (far_sum[...] + from_sib[t, 0].astype(f32)).astype(bf16)
        copies.append(copy(to_far.at[t], from_far.at[t], far))
        give(1, sib_quarter)
        keep(near_quarter, own_sum)
        return copies[1:]

    def reduce_end(t, copies, own_sum, from_sib, from_far):
        wait_all(copies)

        def grad_of(place):
            return (
                own_sum[place, :]
                + from_sib[t, 1, place, :].astype(f32)
                + from_far[t, place, :].astype(f32)
            )

        return grad_of

    def rel_begin(t):
        pairs = half_rows // LANES

        def store(place, value):
            rel_to_sib[t, place, :] = value.astype(bf16)

        scatter(t, rel_at, edges, (1 - core) * pairs, pairs, grad_rel, store)
        swap = copy(rel_to_sib.at[t], rel_from_sib.at[t], sibling)

        def keep(place, value):
            rel_own_sum[place, :] = value

        scatter(t, rel_at, edges, core * pairs, pairs, grad_rel, keep)
        return swap

    many = pl.ds(0, (plane - 1) * piece)

    def take_sems():
        index = used[0]
        used[0] += 1
        return send_sems.at[index], recv_sems.at[index]

    def wait_many(t, sem):
        whole = rel_parts.at[t, many]
        pltpu.make_async_copy(whole, whole, sem).wait()

    def rel_spread(t, swap):
        swap.wait_recv()
        sems = take_sems()

        def join(place):
            rel_half[t, place, :] = (
                rel_own_sum[place, :] + rel_from_sib[t, place, :].astype(f32)
            ).astype(bf16)

        def send(k):
            place = rows_of(lax.rem(at_plane + k + 1, plane), piece)
            join(place)
            pltpu.make_async_remote_copy(
                src_ref=rel_half.at[t, place],
                dst_ref=rel_parts.at[t, rows_of(k, piece)],
                send_sem=sems[0],
                recv_sem=sems[1],
                device_id=plane_peer(k + 1),
                device_id_type=MESH,
            ).start()

        each(plane - 1, send)
        join(rows_of(at_plane, piece))
        return sems

    def rel_cross(t, sems):
        wait_many(t, sems[1])
        total = rel_half[t, rows_of(at_plane, piece), :].astype(f32)
        for k in range(plane - 1):
            total = total + rel_parts[t, k * piece : (k + 1) * piece, :].astype(f32)
        rel_line[t, at_line] = total.astype(bf16)
        mine = rel_line.at[t, at_line]
        crossed = [copy(mine, mine, line_peer(k)) for k in range(1, line)]
        wait_many(t, sems[0])
        return crossed

    def rel_gather(t, crossed):
        wait_all(crossed)
        total = rel_line[t, 0].astype(f32)
        for k in range(1, line):
            total = total + rel_line[t, k].astype(f32)
        place = rows_of(core * plane + at_plane, piece)
        rel_full[t, place, :] = total.astype(bf16)
        sems = take_sems()

        def send(k):
            pltpu.make_async_remote_copy(
                src_ref=rel_full.at[t, place],
                dst_ref=rel_full.at[t, place],
                send_sem=sems[0],
                recv_sem=sems[1],
                device_id=plane_peer(k + 1),
                device_id_type=MESH,
            ).start()

        each(plane - 1, send)
        return sems

    def rel_back(t, sems):
        wait_many(t, sems[1])
        ours = rows_of(core, half_rows)
        back = copy(rel_full.at[t, ours], rel_full.at[t, ours], sibling)
        wait_many(t, sems[0])
        return back

    def round_relations():
        def block(i):
            place = rows_of(i, CHUNK)
            rel_b[place, :] = rel[place, :].astype(bf16)

        each(rels // CHUNK, block)

    def left_send(t):
        mine = left_all.at[t, rows_of(near_quarter)]
        return copy(mine, mine, far), copy(mine, mine, sibling)

    def left_forward(t, far_copy):
        far_copy.wait_recv()
        theirs = left_all.at[t, rows_of(far_quarter)]
        return copy(theirs, theirs, sibling)

    part = quarter // ROLL_PARTS

    def part_of(index, i):
        return pl.ds(pl.multiple_of(index * quarter + i * part, part), part)

    def right_send(t):
        return [
            copy(
                right_own.at[t, pl.ds(i * part, part)],
                right_all.at[t, part_of(near_quarter, i)],
                following,
            )
            for i in range(ROLL_PARTS)
        ]

    def right_spread(t, rolled):
        to_far, to_sib = [], []
        for i, made in enumerate(rolled):
            made.wait_recv()
            mine = right_all.at[t, part_of(near_quarter, i)]
            to_far.append(copy(mine, mine, far))
            to_sib.append(copy(mine, mine, sibling))
        return to_far, to_sib

    def right_forward(t, to_far):
        forwarded = []
        for i, made in enumerate(to_far):
            made.wait_recv()
            theirs = right_all.at[t, part_of(far_quarter, i)]
            forwarded.append(copy(theirs, theirs, sibling))
        return forwarded

    def wait_all(copies):
        for made in copies:
            made.wait_recv()

    def look_left(t, index, fresh=False):
        lookup(
            t, src_at, edges, index * blocks, blocks, left_all.at[t, rows_of(index)], source, fresh
        )

    def look_right(t, index, fresh=False):
        lookup(
            t,
            target_at,
            targets,
            index * blocks,
            blocks,
            right_all.at[t, rows_of(index)],
            target,
            fresh,
        )

    def look_relation(t):
        lookup(t, rel_at, edges, 0, rels // LANES, rel_b, relation, True)

    def split_right(t, place, value):
        high = value.astype(bf16)
        right_own[t, place, :] = high
        right_low_own[t, place, :] = (value - high.astype(f32)).astype(bf16)

    def right_rows(t):
        def table_of(place):
            start = pl.multiple_of(near_quarter * quarter + place.start, LANES)
            high = right_all[t, pl.ds(start, place.size), :]
            return high.astype(f32) + right_low[t, place, :].astype(f32)

        return table_of

    def keep_left(place, value):
        left[place, :] = value

    def keep_right(place, value):
        right[place, :] = value

    def keep_rel(place, value):
        rel[place, :] = value

    def left_rows(place):
        return left[place, :]

    def rel_rows(place):
        return rel[place, :]

    def rel_grads(place):
        return rel_full[0, place, :].astype(f32)

    def reduce_right(t):
        return reduce_begin(
            t,
            target_at,
            targets,
            grad_target,
            right_to_sib,
            right_from_sib,
            right_far_sum,
            right_own_sum,
            right_to_far,
            right_from_far,
        )

    def reduce_left(t):
        return reduce_begin(
            t,
            src_at,
            edges,
            grad_src,
            left_to_sib,
            left_from_sib,
            left_far_sum,
            left_own_sum,
            left_to_far,
            left_from_far,
        )

    def send_low(t, state):
        return [
            copy(right_low_own.at[t], right_low.at[t], following),
            copy(state, right_state.at[t], following),
        ]

    fetched = [fetch(right_in, right, 0), fetch(left_in, left, 1), fetch(rel_in, rel, 2)]
    barrier = pltpu.get_barrier_semaphore()
    for device in (sibling, following, preceding):
        pl.semaphore_signal(barrier, inc=1, device_id=device, device_id_type=MESH)
    for k in range(1, line):
        pl.semaphore_signal(barrier, inc=1, device_id=line_peer(k), device_id_type=MESH)

    def greet(k):
        pl.semaphore_signal(barrier, inc=1, device_id=plane_peer(k + 1), device_id_type=MESH)

    each(plane - 1, greet)
    fetched[0].wait()
    split_right(0, pl.ds(0, quarter), right[...])
    fetched[1].wait()
    left_all[0, rows_of(near_quarter), :] = left[...].astype(bf16)
    fetched[2].wait()
    round_relations()
    prepare(0)
    pl.semaphore_wait(barrier, 3 + line - 1 + plane - 1)

    rolled = right_send(0)
    left_far, left_sib = left_send(0)
    look_relation(0)
    look_left(0, near_quarter, True)
    left_sib.wait_recv()
    look_left(0, sib_quarter)
    right_far, right_sib = right_spread(0, rolled)
    lows = send_low(0, right_state_in)
    left_far_sib = left_forward(0, left_far)
    look_left(0, far_quarter)
    look_right(0, near_quarter, True)
    left_far_sib.wait_recv()
    look_left(0, far_sib_quarter)
    wait_all(right_sib)
    look_right(0, sib_quarter)
    prepare(1)
    right_far_sib = right_forward(0, right_far)
    look_right(0, far_quarter)
    wait_all(right_far_sib)
    look_right(0, far_sib_quarter)
    dense(0)

    right_copies = reduce_right(0)
    spread = rel_spread(0, rel_begin(0))
    left_copies = reduce_left(0)
    wait_all(lows)
    right_grad = reduce_end(0, right_copies, right_own_sum, right_from_sib, right_from_far)
    update(
        quarter,
        right_rows(0),
        right_state.at[0],
        right_grad,
        functools.partial(split_right, 1),
        right_state_next,
    )
    rolled = right_send(1)
    crossed = rel_cross(0, spread)
    left_grad = reduce_end(0, left_copies, left_own_sum, left_from_sib, left_from_far)
    update(quarter, left_rows, left_state_in, left_grad, keep_left, left_state_out)
    left_all[1, rows_of(near_quarter), :] = left[...].astype(bf16)
    left_far, left_sib = left_send(1)
    gathered = rel_gather(0, crossed)
    right_far, right_sib = right_spread(1, rolled)
    look_left(1, near_quarter, True)
    left_sib.wait_recv()
    look_left(1, sib_quarter)
    left_far_sib = left_forward(1, left_far)
    back = rel_back(0, gathered)
    look_left(1, far_quarter)
    left_far_sib.wait_recv()
    look_left(1, far_sib_quarter)
    back.wait_recv()
    update(rels, rel_rows, rel_state_in, rel_grads, keep_rel, rel_state_out)
    rel_written = fetch(rel, rel_out, 0)
    round_relations()
    look_relation(1)
    look_right(1, near_quarter, True)
    wait_all(right_sib)
    look_right(1, sib_quarter)
    right_far_sib = right_forward(1, right_far)
    lows = send_low(1, right_state_next)
    look_right(1, far_quarter)
    wait_all(right_far_sib)
    look_right(1, far_sib_quarter)
    dense(1)

    spread = rel_spread(1, rel_begin(1))
    right_copies = reduce_right(1)
    left_copies = reduce_left(1)
    crossed = rel_cross(1, spread)
    wait_all(lows)
    right_grad = reduce_end(1, right_copies, right_own_sum, right_from_sib, right_from_far)
    update(quarter, right_rows(1), right_state.at[1], right_grad, keep_right, right_state_out)
    right_written = fetch(right, right_out, 1)
    gathered = rel_gather(1, crossed)
    left_grad = reduce_end(1, left_copies, left_own_sum, left_from_sib, left_from_far)
    update(quarter, left_rows, left_state_out, left_grad, keep_left, left_state_out)
    left_written = fetch(left, left_out, 2)
    back = rel_back(1, gathered)
    ours, theirs = rows_of(core, half_rows), rows_of(1 - core, half_rows)
    ours_written = fetch(rel_full.at[1, ours], rel_grad_out.at[ours], 3)
    back.wait_recv()
    theirs_written = fetch(rel_full.at[1, theirs], rel_grad_out.at[theirs], 4)
    for made in (rel_written, right_written, left_written, ours_written, theirs_written):
        made.wait()
    for made in sent:
        made.wait_send()


def finish(left, left_state, right, right_state, rel, rel_state, rel_grad, *results):
    left_out, left_state_out, right_out, right_state_out, rel_out, rel_state_out = results
    left_out[...] = left[...]
    right_out[...] = right[...]
    left_state_out[...] = left_state[...]
    right_state_out[...] = right_state[...]
    count = rel.shape[0] // LANES
    first = pl.program_id(0) * count
    for i in range(count):
        place = pl.ds(i * LANES, LANES)
        value, row = adagrad(
            rel[place, :], rel_state[pl.ds(first + i, 1), :], rel_grad[place, :].astype(jnp.float32)
        )
        rel_out[place, :] = value
        rel_state_out[pl.ds(first + i, 1), :] = row


def local(
    left_table,
    left_state,
    right_table,
    right_state,
    relations,
    relation_state,
    src_rows,
    dst_rows,
    rel_ids,
    neg_rows,
):
    quarter, width = left_table.shape
    edges = src_rows.shape[1]
    negs = neg_rows.shape[1]
    rels = relations.shape[0]
    slab = quarter * lax.axis_size("edge")
    indices = 3 * edges + negs
    targets = edges + negs
    f32, bf16 = jnp.float32, jnp.bfloat16
    state_shape = (quarter // LANES, LANES)
    rel_state_shape = (rels // LANES, LANES)

    line = 4
    piece = rels // 2 // (lax.axis_size("dom") // 2)

    def vmem(shape, kind):
        return pltpu.VMEM(shape, kind)

    half_rows = rels // 2
    results = pl.pallas_call(
        functools.partial(body, lax.axis_size("dom")),
        out_shape=(
            jax.ShapeDtypeStruct((quarter, width), f32),
            jax.ShapeDtypeStruct(state_shape, f32),
            jax.ShapeDtypeStruct((quarter, width), f32),
            jax.ShapeDtypeStruct(state_shape, f32),
            jax.ShapeDtypeStruct((rels, width), f32),
            jax.ShapeDtypeStruct(rel_state_shape, f32),
            jax.ShapeDtypeStruct((rels, width), bf16),
        ),
        in_specs=[
            pl.BlockSpec(memory_space=pl.ANY if i in (0, 2, 4) else pltpu.VMEM) for i in range(10)
        ],
        out_specs=tuple(
            pl.BlockSpec(memory_space=pl.ANY if i in (0, 2, 4, 6) else pltpu.VMEM) for i in range(7)
        ),
        scratch_shapes=[
            vmem((quarter, width), f32),
            vmem((quarter, width), f32),
            vmem((rels, width), f32),
            vmem((STEPS, indices, LANES), bf16),
            vmem((STEPS, indices, LANES), bf16),
            vmem((STEPS, 16, indices), bf16),
            vmem((STEPS, LANES, indices), bf16),
            vmem((rels, width), bf16),
            vmem((edges, width), f32),
            vmem((targets, width), f32),
            vmem((edges, width), f32),
            vmem((negs, width), bf16),
            vmem((edges, width), bf16),
            vmem((edges, width), bf16),
            vmem((edges, width), bf16),
            vmem((targets, width), bf16),
            vmem((negs, width), f32),
            vmem((STEPS, slab, width), bf16),
            vmem((STEPS, slab, width), bf16),
            vmem((STEPS, quarter, width), bf16),
            vmem((STEPS, quarter, width), bf16),
            vmem((STEPS, quarter, width), bf16),
            vmem((STEPS,) + state_shape, f32),
            vmem(state_shape, f32),
            vmem((quarter, width), f32),
            vmem((quarter, width), f32),
            vmem((quarter, width), f32),
            vmem((quarter, width), f32),
            vmem((half_rows, width), f32),
            vmem((STEPS, 2, quarter, width), bf16),
            vmem((STEPS, 2, quarter, width), bf16),
            vmem((STEPS, quarter, width), bf16),
            vmem((STEPS, quarter, width), bf16),
            vmem((STEPS, 2, quarter, width), bf16),
            vmem((STEPS, 2, quarter, width), bf16),
            vmem((STEPS, quarter, width), bf16),
            vmem((STEPS, quarter, width), bf16),
            vmem((STEPS, half_rows, width), bf16),
            vmem((STEPS, half_rows, width), bf16),
            vmem((STEPS, half_rows, width), bf16),
            vmem((STEPS, half_rows, width), bf16),
            vmem((STEPS, line, piece, width), bf16),
            vmem((STEPS, rels, width), bf16),
            pltpu.SemaphoreType.DMA((64,)),
            pltpu.SemaphoreType.DMA((64,)),
            pltpu.SemaphoreType.DMA((5,)),
        ],
        name="buckets",
        compiler_params=pltpu.CompilerParams(
            collective_id=0, has_side_effects=True, vmem_limit_bytes=56 << 20
        ),
    )(
        left_table,
        left_state.reshape(state_shape),
        right_table,
        right_state.reshape(state_shape),
        relations,
        relation_state.reshape(rel_state_shape),
        src_rows,
        dst_rows,
        rel_ids,
        neg_rows,
    )
    rows = pl.BlockSpec((quarter // FINISH, width), lambda i: (i, 0))
    states = pl.BlockSpec(state_shape, lambda i: (0, 0))
    rel_rows = pl.BlockSpec((rels // FINISH, width), lambda i: (i, 0))
    rel_states = pl.BlockSpec(rel_state_shape, lambda i: (0, 0))
    blocks = (rows, states, rows, states, rel_rows, rel_states)
    left, left_s, right, right_s, rel, rel_s = pl.pallas_call(
        finish,
        grid=(FINISH,),
        out_shape=tuple(jax.ShapeDtypeStruct(r.shape, f32) for r in results[:6]),
        in_specs=list(blocks) + [rel_rows],
        out_specs=blocks,
        name="finish",
        compiler_params=pltpu.CompilerParams(vmem_limit_bytes=32 << 20),
    )(*results)
    return (left, left_s.reshape(-1), right, right_s.reshape(-1), rel, rel_s.reshape(-1))


def solution(mesh):
    placed = (
        P(("dom", "edge"), None),
        P(("dom", "edge")),
        P(("dom", "edge"), None),
        P(("dom", "edge")),
        P(),
        P(),
        P(None, ("dom", "edge")),
        P(None, ("dom", "edge")),
        P(None, ("dom", "edge")),
        P(None, ("dom", "edge")),
    )
    return jax.shard_map(
        local,
        mesh=mesh,
        in_specs=placed,
        out_specs=(
            P(("dom", "edge"), None),
            P(("dom", "edge")),
            P(("dom", "edge"), None),
            P(("dom", "edge")),
            P(),
            P(),
        ),
        check_vma=False,
    )
```

```python
import functools

import jax
import jax.numpy as jnp
from jax import lax
from jax.experimental import pallas as pl
from jax.experimental.pallas import tpu as pltpu
from jax.sharding import PartitionSpec as P

STEPS = 2
LANES = 128
CHUNK = 256
PARTS = 4
LEFT_PARTS = 2
REL_PARTS = 2
FINISH = 2
MESH = pl.DeviceIdType.MESH
learn_rate = 0.1
neg_weight = 0.0625


def eye(kind=jnp.float32):
    rows = lax.broadcasted_iota(jnp.int32, (LANES, LANES), 0)
    columns = lax.broadcasted_iota(jnp.int32, (LANES, LANES), 1)
    return rows == columns


def to_column(row):
    spread = jnp.where(eye(), jnp.broadcast_to(row, (LANES, LANES)), 0.0)
    return jnp.sum(spread, axis=1, keepdims=True)


def to_row(column):
    spread = jnp.where(eye(), jnp.broadcast_to(column, (LANES, LANES)), 0.0)
    return jnp.sum(spread, axis=0, keepdims=True)


def adagrad(table, state, grad):
    column = to_column(state) + jnp.mean(grad * grad, axis=1, keepdims=True)
    return table - learn_rate * grad / jnp.sqrt(column), to_row(column)


def body(
    n_dom,
    left_in,
    left_state_in,
    right_in,
    right_state_in,
    rel_in,
    rel_state_in,
    src_rows,
    dst_rows,
    rel_rows,
    neg_rows,
    left_out,
    left_state_out,
    right_out,
    right_state_out,
    rel_out,
    rel_state_out,
    rel_grad_out,
    left,
    left_state,
    right,
    right_state_first,
    rel,
    rel_state,
    src_in,
    dst_in,
    rel_ids_in,
    neg_in,
    high_col,
    low_col,
    high_row,
    low_row,
    rel_b,
    source,
    target,
    relation,
    negatives,
    product_b,
    grad_src,
    grad_rel,
    grad_target,
    grad_neg_acc,
    left_all,
    right_all,
    right_own,
    right_low_own,
    right_low,
    right_state,
    right_state_next,
    right_state_last,
    left_far_sum,
    left_own_sum,
    right_far_sum,
    right_own_sum,
    rel_own_sum,
    left_to_sib,
    left_from_sib,
    left_to_far,
    left_from_far,
    right_to_sib,
    right_from_sib,
    right_to_far,
    right_from_far,
    rel_to_sib,
    rel_from_sib,
    rel_half,
    rel_parts,
    rel_line,
    rel_full,
    send_sems,
    recv_sems,
    local_sems,
):
    f32, bf16 = jnp.float32, jnp.bfloat16
    quarter, width = left_in.shape
    edges = src_in.shape[1]
    negs = neg_in.shape[1]
    rels = rel_in.shape[0]
    half_dim = width // 2
    blocks = quarter // LANES
    half_rows = rels // 2
    n_y = 4 if n_dom % 8 == 0 else 2
    n_low = 2
    n_z = n_dom // (n_y * n_low)
    plane = n_z * n_y
    line = 2 * n_low
    piece = half_rows // plane // REL_PARTS
    rel_part = half_rows // REL_PARTS
    src_at, rel_at, target_at = 0, edges, 2 * edges
    targets = edges + negs

    p = lax.axis_index("dom")
    e = lax.axis_index("edge")
    core = lax.rem(e, 2)
    side = e // 2
    z, x_low, y = p // (n_y * n_low), lax.rem(p // n_y, n_low), lax.rem(p, n_y)
    at_plane = z * n_y + y
    at_line = side * n_low + x_low
    sibling = (p, side * 2 + 1 - core)
    far = (p, (1 - side) * 2 + core)
    following = (lax.rem(p + 1, n_dom), e)
    preceding = (lax.rem(p + n_dom - 1, n_dom), e)
    near_quarter = side * 2 + core
    sib_quarter = side * 2 + 1 - core
    far_quarter = (1 - side) * 2 + core
    far_sib_quarter = (1 - side) * 2 + 1 - core

    def plane_peer(k):
        g = lax.rem(at_plane + k, plane)
        return (g // n_y * (n_y * n_low) + x_low * n_y + lax.rem(g, n_y), e)

    def line_peer(k):
        g = lax.rem(at_line + k, line)
        return (z * (n_y * n_low) + lax.rem(g, n_low) * n_y + y, g // n_low * 2 + core)

    def rows_of(index, size=quarter):
        return pl.ds(pl.multiple_of(index * size, size), size)

    used = [0]
    sent = []

    def take(count=1):
        index = used[0]
        used[0] += count
        return index

    def describe(source_ref, target_ref, device, send_index, recv_index):
        return pltpu.make_async_remote_copy(
            src_ref=source_ref,
            dst_ref=target_ref,
            send_sem=send_sems.at[send_index],
            recv_sem=recv_sems.at[recv_index],
            device_id=device,
            device_id_type=MESH,
        )

    def copy(source_ref, target_ref, device):
        index = take()
        made = describe(source_ref, target_ref, device, index, index)
        made.start()
        sent.append(made)
        return made

    def each(count, step):
        def run(i, carry):
            step(i)
            return carry

        lax.fori_loop(0, count, run, 0)

    def prepare(t):
        lists = (
            (src_in, src_at, edges),
            (rel_ids_in, rel_at, edges),
            (dst_in, target_at, edges),
            (neg_in, target_at + edges, negs),
        )
        for ref, at, count in lists:

            def block(j, ref=ref, at=at):
                row = ref[t : t + 1, pl.ds(pl.multiple_of(j * LANES, LANES), LANES)]
                place = pl.ds(pl.multiple_of(at + j * LANES, LANES), LANES)
                high = (row >> 7).astype(f32)
                low = (row & 127).astype(f32)
                lanes = lax.broadcasted_iota(jnp.int32, (LANES, LANES), 1).astype(f32)
                subs = lax.broadcasted_iota(jnp.int32, (LANES, LANES), 0).astype(f32)
                low_row[t, :, place] = jnp.where(subs == low, 1.0, 0.0).astype(bf16)
                high_row[t, :, place] = jnp.broadcast_to(high, (16, LANES)).astype(bf16)
                column = jnp.broadcast_to(to_column(row.astype(f32)), (LANES, LANES))
                high_c = jnp.floor(column * (1.0 / LANES))
                low_c = column - LANES * high_c
                high_col[t, place, :] = high_c.astype(bf16)
                low_col[t, place, :] = jnp.where(lanes == low_c, 1.0, 0.0).astype(bf16)

            for j in range(count // LANES):
                block(j)

    def level(index, shape):
        return jnp.full(shape, jnp.asarray(index, jnp.int32).astype(f32), f32).astype(bf16)

    def lookup(t, at, count, first_block, n_blocks, table, out, fresh):
        def chunk(i):
            place = pl.ds(pl.multiple_of(at + i * CHUNK, CHUNK), CHUNK)
            high = high_col[t, place, :]
            low = low_col[t, place, :]
            zero = jnp.zeros_like(low)
            matches = jnp.concatenate(
                [
                    jnp.where(high == level(first_block + j, high.shape), low, zero)
                    for j in range(n_blocks)
                ],
                axis=1,
            )
            found = jnp.dot(matches, table[...], preferred_element_type=f32)
            dest = pl.ds(pl.multiple_of(i * CHUNK, CHUNK), CHUNK)
            if fresh:
                out[dest, :] = found
            else:
                out[dest, :] += found

        for i in range(count // CHUNK):
            chunk(i)

    def scatter(t, at, count, first_block, n_blocks, values, store):
        def pair(i):
            high = high_row[t, :, at : at + count]
            low = low_row[t, :, at : at + count]
            one, none = jnp.ones_like(high), jnp.zeros_like(high)
            parts = []
            for j in range(2):
                hit = jnp.where(high == level(first_block + 2 * i + j, high.shape), one, none)
                parts.append(low * jnp.concatenate([hit] * (LANES // 16), axis=0))
            matches = jnp.concatenate(parts, axis=0)
            store(
                pl.ds(pl.multiple_of(i * 2 * LANES, 2 * LANES), 2 * LANES),
                jnp.dot(matches, values[...], preferred_element_type=f32),
            )

        for i in range(n_blocks // 2):
            pair(i)

    def dense(t):
        negatives[...] = target[edges:, :].astype(bf16)
        grad_neg_acc[...] = jnp.zeros_like(grad_neg_acc)

        def chunk(i):
            place = pl.ds(pl.multiple_of(i * CHUNK, CHUNK), CHUNK)
            s_re, s_im = source[place, :half_dim], source[place, half_dim:]
            r_re, r_im = relation[place, :half_dim], relation[place, half_dim:]
            goal = target[place, :]
            product = jnp.concatenate(
                [s_re * r_re - s_im * r_im, s_re * r_im + s_im * r_re], axis=1
            )
            positive = jnp.sum(product * goal, axis=1, keepdims=True)
            rounded = product.astype(bf16)
            product_b[place, :] = rounded
            n_b = negatives[...]
            negative = lax.dot_general(
                rounded, n_b, (((1,), (1,)), ((), ())), preferred_element_type=f32
            )
            g_pos = -1.0 / (1.0 + jnp.exp(positive))
            g_neg = (neg_weight / (1.0 + jnp.exp(-negative))).astype(bf16)
            g_q = g_pos * goal + jnp.dot(g_neg, n_b, preferred_element_type=f32)
            g_re, g_im = g_q[:, :half_dim], g_q[:, half_dim:]
            grad_src[place, :half_dim] = (g_re * r_re + g_im * r_im).astype(bf16)
            grad_src[place, half_dim:] = (g_im * r_re - g_re * r_im).astype(bf16)
            grad_rel[place, :half_dim] = (g_re * s_re + g_im * s_im).astype(bf16)
            grad_rel[place, half_dim:] = (g_im * s_re - g_re * s_im).astype(bf16)
            grad_target[place, :] = (g_pos * product).astype(bf16)
            grad_neg_acc[...] += lax.dot_general(
                g_neg, rounded, (((0,), (0,)), ((), ())), preferred_element_type=f32
            )

        each(edges // CHUNK, chunk)
        grad_target[edges:, :] = grad_neg_acc[...].astype(bf16)

    def fetch(source_ref, target_ref, index):
        made = pltpu.make_async_copy(source_ref, target_ref, local_sems.at[index])
        made.start()
        return made

    def update_block(i, table_of, state, grad_of, store, state_to):
        place = pl.ds(i * LANES, LANES)
        value, row = adagrad(table_of(place), state[i : i + 1, :], grad_of(place))
        store(place, value)
        state_to[i : i + 1, :] = row

    def reduce_begin(t, at, count, values, to_sib, from_sib, far_sum, own_sum, to_far, from_far):
        copies = []

        def give(i, quarter_index):
            def store(place, value):
                to_sib[t, i, place, :] = value.astype(bf16)

            scatter(t, at, count, quarter_index * blocks, blocks, values, store)
            copies.append(copy(to_sib.at[t, i], from_sib.at[t, i], sibling))

        def keep(quarter_index, total):
            def store(place, value):
                total[place, :] = value

            scatter(t, at, count, quarter_index * blocks, blocks, values, store)

        give(0, far_sib_quarter)
        keep(far_quarter, far_sum)
        copies[0].wait_recv()
        for i in range(PARTS):
            place = pl.ds(i * part, part)
            to_far[t, place, :] = (
                far_sum[place, :] + from_sib[t, 0, place, :].astype(f32)
            ).astype(bf16)
            copies.append(copy(to_far.at[t, place], from_far.at[t, place], far))
        give(1, sib_quarter)
        keep(near_quarter, own_sum)
        return copies[1:]

    def reduce_end(t, copies, own_sum, from_sib, from_far, apply):
        copies[-1].wait_recv()

        def grad_of(place):
            return (
                own_sum[place, :]
                + from_sib[t, 1, place, :].astype(f32)
                + from_far[t, place, :].astype(f32)
            )

        for i in range(PARTS):
            copies[i].wait_recv()
            for j in range(part // LANES):
                apply(i * (part // LANES) + j, grad_of)

    def rel_begin(t):
        pairs = rel_part // LANES
        swaps = []
        for h in range(REL_PARTS):

            def store(place, value, h=h):
                rel_to_sib[t, pl.ds(h * rel_part + place.start, place.size), :] = value.astype(bf16)

            first = ((1 - core) * REL_PARTS + h) * pairs
            scatter(t, rel_at, edges, first, pairs, grad_rel, store)
            span = pl.ds(h * rel_part, rel_part)
            swaps.append(copy(rel_to_sib.at[t, span], rel_from_sib.at[t, span], sibling))
        for h in range(REL_PARTS):

            def keep(place, value, h=h):
                rel_own_sum[pl.ds(h * rel_part + place.start, place.size), :] = value

            scatter(t, rel_at, edges, (core * REL_PARTS + h) * pairs, pairs, grad_rel, keep)
        return swaps

    many = pl.ds(0, (plane - 1) * piece)

    def wait_many(t, h, sem):
        whole = rel_parts.at[t, h, many]
        pltpu.make_async_copy(whole, whole, sem).wait()

    def rel_span(h, index):
        return pl.ds(pl.multiple_of(h * rel_part + index * piece, piece), piece)

    def rel_spread(t, swaps):
        indices = []
        for h in range(REL_PARTS):
            swaps[h].wait_recv()
            index = take()
            indices.append(index)

            def join(place):
                rel_half[t, place, :] = (
                    rel_own_sum[place, :] + rel_from_sib[t, place, :].astype(f32)
                ).astype(bf16)

            def send(k, h=h, index=index):
                place = rel_span(h, lax.rem(at_plane + k + 1, plane))
                join(place)
                describe(
                    rel_half.at[t, place],
                    rel_parts.at[t, h, rows_of(k, piece)],
                    plane_peer(k + 1),
                    index,
                    index,
                ).start()

            each(plane - 1, send)
            join(rel_span(h, at_plane))
        return indices

    def rel_cross(t, h, indices):
        wait_many(t, h, recv_sems.at[indices[h]])
        total = rel_half[t, rel_span(h, at_plane), :].astype(f32)
        for k in range(plane - 1):
            total = total + rel_parts[t, h, k * piece : (k + 1) * piece, :].astype(f32)
        rel_line[t, h, at_line] = total.astype(bf16)
        mine = rel_line.at[t, h, at_line]
        crossed = [copy(mine, mine, line_peer(k)) for k in range(1, line)]
        wait_many(t, h, send_sems.at[indices[h]])
        return crossed

    def rel_gather(t, h, crossed):
        wait_all(crossed)
        total = rel_line[t, h, 0].astype(f32)
        for k in range(1, line):
            total = total + rel_line[t, h, k].astype(f32)
        start = core * half_rows + h * rel_part + at_plane * piece
        place = pl.ds(pl.multiple_of(start, piece), piece)
        rel_full[t, place, :] = total.astype(bf16)
        index = take()

        def send(k):
            mine = rel_full.at[t, place]
            describe(mine, mine, plane_peer(k + 1), index, index).start()

        each(plane - 1, send)
        return index

    def rel_rows_of(which, h):
        start = which * half_rows + h * rel_part
        return pl.ds(pl.multiple_of(start, rel_part), rel_part)

    def rel_back(t, h, index):
        wait_many(t, h, recv_sems.at[index])
        ours = rel_full.at[t, rel_rows_of(core, h)]
        back = copy(ours, ours, sibling)
        wait_many(t, h, send_sems.at[index])
        return back

    def round_relations():
        def block(i):
            place = rows_of(i, CHUNK)
            rel_b[place, :] = rel[place, :].astype(bf16)

        each(rels // CHUNK, block)

    part = quarter // PARTS
    left_part = quarter // LEFT_PARTS

    def part_of(index, i, size):
        return pl.ds(pl.multiple_of(index * quarter + i * size, size), size)

    def left_send(t, i):
        mine = left_all.at[t, part_of(near_quarter, i, left_part)]
        return copy(mine, mine, far), copy(mine, mine, sibling)

    def left_forward(t, far_copies):
        forwarded = []
        for i, made in enumerate(far_copies):
            made.wait_recv()
            theirs = left_all.at[t, part_of(far_quarter, i, left_part)]
            forwarded.append(copy(theirs, theirs, sibling))
        return forwarded

    def right_send(t, i):
        mine = right_own.at[t, pl.ds(i * part, part)]
        return copy(mine, right_all.at[t, part_of(near_quarter, i, part)], following)

    def right_spread(t, rolled):
        to_far, to_sib = [], []
        for i, made in enumerate(rolled):
            made.wait_recv()
            mine = right_all.at[t, part_of(near_quarter, i, part)]
            to_far.append(copy(mine, mine, far))
            to_sib.append(copy(mine, mine, sibling))
        return to_far, to_sib

    def right_forward(t, to_far):
        forwarded = []
        for i, made in enumerate(to_far):
            made.wait_recv()
            theirs = right_all.at[t, part_of(far_quarter, i, part)]
            forwarded.append(copy(theirs, theirs, sibling))
        return forwarded

    def wait_all(copies):
        for made in copies:
            made.wait_recv()

    def look_left(t, index, fresh=False):
        lookup(
            t, src_at, edges, index * blocks, blocks, left_all.at[t, rows_of(index)], source, fresh
        )

    def look_right(t, index, fresh=False):
        lookup(
            t,
            target_at,
            targets,
            index * blocks,
            blocks,
            right_all.at[t, rows_of(index)],
            target,
            fresh,
        )

    def look_relation(t):
        lookup(t, rel_at, edges, 0, rels // LANES, rel_b, relation, True)

    def split_right(t, place, value):
        high = value.astype(bf16)
        right_own[t, place, :] = high
        right_low_own[t, place, :] = (value - high.astype(f32)).astype(bf16)

    def right_rows(t):
        def table_of(place):
            start = pl.multiple_of(near_quarter * quarter + place.start, LANES)
            high = right_all[t, pl.ds(start, place.size), :]
            return high.astype(f32) + right_low[t, place, :].astype(f32)

        return table_of

    def keep_left(place, value):
        left[place, :] = value

    def keep_right(place, value):
        right[place, :] = value

    def keep_rel(place, value):
        rel[place, :] = value

    def left_rows(place):
        return left[place, :]

    def rel_values(place):
        return rel[place, :]

    def rel_grads(place):
        return rel_full[0, place, :].astype(f32)

    def reduce_right(t):
        return reduce_begin(
            t,
            target_at,
            targets,
            grad_target,
            right_to_sib,
            right_from_sib,
            right_far_sum,
            right_own_sum,
            right_to_far,
            right_from_far,
        )

    def reduce_left(t):
        return reduce_begin(
            t,
            src_at,
            edges,
            grad_src,
            left_to_sib,
            left_from_sib,
            left_far_sum,
            left_own_sum,
            left_to_far,
            left_from_far,
        )

    def send_low(t, state):
        return [
            copy(right_low_own.at[t], right_low.at[t], following),
            copy(state, right_state.at[t], following),
        ]

    pairs = (
        (right_in, right),
        (left_in, left),
        (rel_in, rel),
        (rel_rows, rel_ids_in),
        (src_rows, src_in),
        (dst_rows, dst_in),
        (neg_rows, neg_in),
        (right_state_in, right_state_first),
        (left_state_in, left_state),
        (rel_state_in, rel_state),
    )
    barrier = pltpu.get_barrier_semaphore()
    greeted = [sibling, following, preceding]
    greeted += [line_peer(k) for k in range(1, line)]
    for device in greeted:
        pl.semaphore_signal(barrier, inc=1, device_id=device, device_id_type=MESH)

    def greet(k):
        pl.semaphore_signal(barrier, inc=1, device_id=plane_peer(k + 1), device_id_type=MESH)

    each(plane - 1, greet)
    fetched = [fetch(a, b, i) for i, (a, b) in enumerate(pairs)]
    fetched[0].wait()
    split_right(0, pl.ds(0, quarter), right[...])
    fetched[1].wait()
    left_all[0, rows_of(near_quarter), :] = left[...].astype(bf16)
    pl.semaphore_wait(barrier, len(greeted) + plane - 1)

    rolled = [right_send(0, i) for i in range(PARTS)]
    left_far, left_sib = zip(*[left_send(0, i) for i in range(LEFT_PARTS)])
    for made in fetched[2:]:
        made.wait()
    round_relations()
    prepare(0)
    look_left(0, near_quarter, True)
    wait_all(left_sib)
    look_left(0, sib_quarter)
    right_far, right_sib = right_spread(0, rolled)
    left_far_sib = left_forward(0, left_far)
    look_relation(0)
    look_left(0, far_quarter)
    look_right(0, near_quarter, True)
    wait_all(left_far_sib)
    look_left(0, far_sib_quarter)
    wait_all(right_sib)
    look_right(0, sib_quarter)
    prepare(1)
    right_far_sib = right_forward(0, right_far)
    lows = send_low(0, right_state_first)
    look_right(0, far_quarter)
    wait_all(right_far_sib)
    look_right(0, far_sib_quarter)
    dense(0)

    right_copies = reduce_right(0)
    spread = rel_spread(0, rel_begin(0))
    left_copies = reduce_left(0)
    wait_all(lows)
    rolled = []

    def next_right(i, grad_of):
        update_block(
            i,
            right_rows(0),
            right_state.at[0],
            grad_of,
            functools.partial(split_right, 1),
            right_state_next,
        )
        if (i + 1) % (part // LANES) == 0:
            rolled.append(right_send(1, i // (part // LANES)))

    reduce_end(0, right_copies, right_own_sum, right_from_sib, right_from_far, next_right)
    crossed = [rel_cross(0, 0, spread)]
    left_sent = []

    def next_left(i, grad_of):
        update_block(i, left_rows, left_state, grad_of, keep_left, left_state)
        block = pl.ds(i * LANES, LANES)
        left_all[1, part_of(near_quarter, i, LANES), :] = left[block, :].astype(bf16)
        if (i + 1) % (left_part // LANES) == 0:
            left_sent.append(left_send(1, i // (left_part // LANES)))

    reduce_end(0, left_copies, left_own_sum, left_from_sib, left_from_far, next_left)
    left_far, left_sib = zip(*left_sent)
    crossed += [rel_cross(0, h, spread) for h in range(1, REL_PARTS)]
    gathered = [rel_gather(0, 0, crossed[0])]
    right_far, right_sib = right_spread(1, rolled)
    gathered += [rel_gather(0, h, crossed[h]) for h in range(1, REL_PARTS)]
    look_left(1, near_quarter, True)
    wait_all(left_sib)
    look_left(1, sib_quarter)
    left_far_sib = left_forward(1, left_far)
    back = [rel_back(0, h, gathered[h]) for h in range(REL_PARTS)]
    look_left(1, far_quarter)
    wait_all(left_far_sib)
    look_left(1, far_sib_quarter)
    wait_all(back)
    for i in range(rels // LANES):
        update_block(i, rel_values, rel_state, rel_grads, keep_rel, rel_state)
    rel_written = [fetch(rel, rel_out, 0), fetch(rel_state, rel_state_out, 1)]
    round_relations()
    look_relation(1)
    look_right(1, near_quarter, True)
    wait_all(right_sib)
    look_right(1, sib_quarter)
    right_far_sib = right_forward(1, right_far)
    lows = send_low(1, right_state_next)
    look_right(1, far_quarter)
    wait_all(right_far_sib)
    look_right(1, far_sib_quarter)
    dense(1)

    spread = rel_spread(1, rel_begin(1))
    right_copies = reduce_right(1)
    left_copies = reduce_left(1)
    crossed = [rel_cross(1, h, spread) for h in range(REL_PARTS)]
    gathered = [rel_gather(1, h, crossed[h]) for h in range(REL_PARTS)]
    wait_all(lows)

    def last_right(i, grad_of):
        update_block(
            i, right_rows(1), right_state.at[1], grad_of, keep_right, right_state_last
        )

    reduce_end(1, right_copies, right_own_sum, right_from_sib, right_from_far, last_right)
    written = [fetch(right, right_out, 2), fetch(right_state_last, right_state_out, 3)]

    def last_left(i, grad_of):
        update_block(i, left_rows, left_state, grad_of, keep_left, left_state)

    reduce_end(1, left_copies, left_own_sum, left_from_sib, left_from_far, last_left)
    written += [fetch(left, left_out, 4), fetch(left_state, left_state_out, 5)]
    back = []
    for h in range(REL_PARTS):
        back.append(rel_back(1, h, gathered[h]))
        ours = rel_rows_of(core, h)
        written.append(fetch(rel_full.at[1, ours], rel_grad_out.at[ours], 6 + 2 * h))
    for h in range(REL_PARTS):
        back[h].wait_recv()
        theirs = rel_rows_of(1 - core, h)
        written.append(fetch(rel_full.at[1, theirs], rel_grad_out.at[theirs], 7 + 2 * h))
    for made in rel_written + written:
        made.wait()
    for made in sent:
        made.wait_send()


def finish(left, left_state, right, right_state, rel, rel_state, rel_grad, *results):
    left_out, left_state_out, right_out, right_state_out, rel_out, rel_state_out = results
    left_out[...] = left[...]
    right_out[...] = right[...]
    left_state_out[...] = left_state[...]
    right_state_out[...] = right_state[...]
    count = rel.shape[0] // LANES
    first = pl.program_id(0) * count
    for i in range(count):
        place = pl.ds(i * LANES, LANES)
        value, row = adagrad(
            rel[place, :], rel_state[pl.ds(first + i, 1), :], rel_grad[place, :].astype(jnp.float32)
        )
        rel_out[place, :] = value
        rel_state_out[pl.ds(first + i, 1), :] = row


def local(
    left_table,
    left_state,
    right_table,
    right_state,
    relations,
    relation_state,
    src_rows,
    dst_rows,
    rel_ids,
    neg_rows,
):
    quarter, width = left_table.shape
    edges = src_rows.shape[1]
    negs = neg_rows.shape[1]
    rels = relations.shape[0]
    slab = quarter * lax.axis_size("edge")
    indices = 3 * edges + negs
    targets = edges + negs
    f32, bf16 = jnp.float32, jnp.bfloat16
    state_shape = (quarter // LANES, LANES)
    rel_state_shape = (rels // LANES, LANES)

    line = 4
    piece = rels // 2 // (lax.axis_size("dom") // 2) // REL_PARTS

    def vmem(shape, kind):
        return pltpu.VMEM(shape, kind)

    half_rows = rels // 2
    results = pl.pallas_call(
        functools.partial(body, lax.axis_size("dom")),
        out_shape=(
            jax.ShapeDtypeStruct((quarter, width), f32),
            jax.ShapeDtypeStruct(state_shape, f32),
            jax.ShapeDtypeStruct((quarter, width), f32),
            jax.ShapeDtypeStruct(state_shape, f32),
            jax.ShapeDtypeStruct((rels, width), f32),
            jax.ShapeDtypeStruct(rel_state_shape, f32),
            jax.ShapeDtypeStruct((rels, width), bf16),
        ),
        in_specs=[pl.BlockSpec(memory_space=pl.ANY)] * 10,
        out_specs=tuple([pl.BlockSpec(memory_space=pl.ANY)] * 7),
        scratch_shapes=[
            vmem((quarter, width), f32),
            vmem(state_shape, f32),
            vmem((quarter, width), f32),
            vmem(state_shape, f32),
            vmem((rels, width), f32),
            vmem(rel_state_shape, f32),
            vmem(src_rows.shape, jnp.int32),
            vmem(dst_rows.shape, jnp.int32),
            vmem(rel_ids.shape, jnp.int32),
            vmem(neg_rows.shape, jnp.int32),
            vmem((STEPS, indices, LANES), bf16),
            vmem((STEPS, indices, LANES), bf16),
            vmem((STEPS, 16, indices), bf16),
            vmem((STEPS, LANES, indices), bf16),
            vmem((rels, width), bf16),
            vmem((edges, width), f32),
            vmem((targets, width), f32),
            vmem((edges, width), f32),
            vmem((negs, width), bf16),
            vmem((edges, width), bf16),
            vmem((edges, width), bf16),
            vmem((edges, width), bf16),
            vmem((targets, width), bf16),
            vmem((negs, width), f32),
            vmem((STEPS, slab, width), bf16),
            vmem((STEPS, slab, width), bf16),
            vmem((STEPS, quarter, width), bf16),
            vmem((STEPS, quarter, width), bf16),
            vmem((STEPS, quarter, width), bf16),
            vmem((STEPS,) + state_shape, f32),
            vmem(state_shape, f32),
            vmem(state_shape, f32),
            vmem((quarter, width), f32),
            vmem((quarter, width), f32),
            vmem((quarter, width), f32),
            vmem((quarter, width), f32),
            vmem((half_rows, width), f32),
            vmem((STEPS, 2, quarter, width), bf16),
            vmem((STEPS, 2, quarter, width), bf16),
            vmem((STEPS, quarter, width), bf16),
            vmem((STEPS, quarter, width), bf16),
            vmem((STEPS, 2, quarter, width), bf16),
            vmem((STEPS, 2, quarter, width), bf16),
            vmem((STEPS, quarter, width), bf16),
            vmem((STEPS, quarter, width), bf16),
            vmem((STEPS, half_rows, width), bf16),
            vmem((STEPS, half_rows, width), bf16),
            vmem((STEPS, half_rows, width), bf16),
            vmem((STEPS, REL_PARTS, half_rows // REL_PARTS, width), bf16),
            vmem((STEPS, REL_PARTS, line, piece, width), bf16),
            vmem((STEPS, rels, width), bf16),
            pltpu.SemaphoreType.DMA((160,)),
            pltpu.SemaphoreType.DMA((160,)),
            pltpu.SemaphoreType.DMA((10,)),
        ],
        name="buckets",
        compiler_params=pltpu.CompilerParams(
            collective_id=0, has_side_effects=True, vmem_limit_bytes=56 << 20
        ),
    )(
        left_table,
        left_state.reshape(state_shape),
        right_table,
        right_state.reshape(state_shape),
        relations,
        relation_state.reshape(rel_state_shape),
        src_rows,
        dst_rows,
        rel_ids,
        neg_rows,
    )
    rows = pl.BlockSpec((quarter // FINISH, width), lambda i: (i, 0))
    states = pl.BlockSpec(state_shape, lambda i: (0, 0))
    rel_rows = pl.BlockSpec((rels // FINISH, width), lambda i: (i, 0))
    rel_states = pl.BlockSpec(rel_state_shape, lambda i: (0, 0))
    blocks = (rows, states, rows, states, rel_rows, rel_states)
    left, left_s, right, right_s, rel, rel_s = pl.pallas_call(
        finish,
        grid=(FINISH,),
        out_shape=tuple(jax.ShapeDtypeStruct(r.shape, f32) for r in results[:6]),
        in_specs=list(blocks) + [rel_rows],
        out_specs=blocks,
        name="finish",
        compiler_params=pltpu.CompilerParams(vmem_limit_bytes=56 << 20),
    )(*results)
    return (left, left_s.reshape(-1), right, right_s.reshape(-1), rel, rel_s.reshape(-1))


def solution(mesh):
    placed = (
        P(("dom", "edge"), None),
        P(("dom", "edge")),
        P(("dom", "edge"), None),
        P(("dom", "edge")),
        P(),
        P(),
        P(None, ("dom", "edge")),
        P(None, ("dom", "edge")),
        P(None, ("dom", "edge")),
        P(None, ("dom", "edge")),
    )
    return jax.shard_map(
        local,
        mesh=mesh,
        in_specs=placed,
        out_specs=(
            P(("dom", "edge"), None),
            P(("dom", "edge")),
            P(("dom", "edge"), None),
            P(("dom", "edge")),
            P(),
            P(),
        ),
        check_vma=False,
    )
```

```python
import functools

import jax
import jax.numpy as jnp
from jax import lax
from jax.experimental import pallas as pl
from jax.experimental.pallas import tpu as pltpu
from jax.sharding import PartitionSpec as P

STEPS = 2
LANES = 128
CHUNK = 256
PARTS = 4
LEFT_PARTS = 2
REL_PARTS = 2
FINISH = 2
MESH = pl.DeviceIdType.MESH
learn_rate = 0.1
neg_weight = 0.0625


def eye(kind=jnp.float32):
    rows = lax.broadcasted_iota(jnp.int32, (LANES, LANES), 0)
    columns = lax.broadcasted_iota(jnp.int32, (LANES, LANES), 1)
    return rows == columns


def to_column(row):
    spread = jnp.where(eye(), jnp.broadcast_to(row, (LANES, LANES)), 0.0)
    return jnp.sum(spread, axis=1, keepdims=True)


def to_row(column):
    spread = jnp.where(eye(), jnp.broadcast_to(column, (LANES, LANES)), 0.0)
    return jnp.sum(spread, axis=0, keepdims=True)


def adagrad(table, state, grad):
    column = to_column(state) + jnp.mean(grad * grad, axis=1, keepdims=True)
    return table - learn_rate * grad / jnp.sqrt(column), to_row(column)


def body(
    n_dom,
    left_in,
    left_state_in,
    right_in,
    right_state_in,
    rel_in,
    rel_state_in,
    src_rows,
    dst_rows,
    rel_rows,
    neg_rows,
    left_out,
    left_state_out,
    right_out,
    right_state_out,
    rel_out,
    rel_state_out,
    rel_grad_out,
    left,
    left_state,
    right,
    right_state_first,
    rel,
    rel_state,
    src_in,
    dst_in,
    rel_ids_in,
    neg_in,
    high_col,
    low_col,
    high_row,
    low_row,
    rel_b,
    source,
    target,
    relation,
    negatives,
    product_b,
    grad_src,
    grad_rel,
    grad_target,
    grad_neg_acc,
    left_all,
    right_all,
    right_own,
    right_low_own,
    right_low,
    right_state,
    right_state_next,
    right_state_last,
    left_far_sum,
    left_own_sum,
    right_far_sum,
    right_own_sum,
    rel_own_sum,
    left_to_sib,
    left_from_sib,
    left_to_far,
    left_from_far,
    right_to_sib,
    right_from_sib,
    right_to_far,
    right_from_far,
    rel_to_sib,
    rel_from_sib,
    rel_half,
    rel_parts,
    rel_line,
    rel_full,
    send_sems,
    recv_sems,
    local_sems,
):
    f32, bf16 = jnp.float32, jnp.bfloat16
    quarter, width = left_in.shape
    edges = src_in.shape[1]
    negs = neg_in.shape[1]
    rels = rel_in.shape[0]
    half_dim = width // 2
    blocks = quarter // LANES
    half_rows = rels // 2
    n_y = 4 if n_dom % 8 == 0 else 2
    n_low = 2
    n_z = n_dom // (n_y * n_low)
    plane = n_z * n_y
    line = 2 * n_low
    piece = half_rows // plane // REL_PARTS
    rel_part = half_rows // REL_PARTS
    src_at, rel_at, target_at = 0, edges, 2 * edges
    targets = edges + negs

    p = lax.axis_index("dom")
    e = lax.axis_index("edge")
    core = lax.rem(e, 2)
    side = e // 2
    z, x_low, y = p // (n_y * n_low), lax.rem(p // n_y, n_low), lax.rem(p, n_y)
    at_plane = z * n_y + y
    at_line = side * n_low + x_low
    sibling = (p, side * 2 + 1 - core)
    far = (p, (1 - side) * 2 + core)
    following = (lax.rem(p + 1, n_dom), e)
    preceding = (lax.rem(p + n_dom - 1, n_dom), e)
    near_quarter = side * 2 + core
    sib_quarter = side * 2 + 1 - core
    far_quarter = (1 - side) * 2 + core
    far_sib_quarter = (1 - side) * 2 + 1 - core

    def plane_peer(k):
        g = lax.rem(at_plane + k, plane)
        return (g // n_y * (n_y * n_low) + x_low * n_y + lax.rem(g, n_y), e)

    def line_peer(k):
        g = lax.rem(at_line + k, line)
        return (z * (n_y * n_low) + lax.rem(g, n_low) * n_y + y, g // n_low * 2 + core)

    def rows_of(index, size=quarter):
        return pl.ds(pl.multiple_of(index * size, size), size)

    used = [0]
    sent = []

    def take(count=1):
        index = used[0]
        used[0] += count
        return index

    def describe(source_ref, target_ref, device, send_index, recv_index):
        return pltpu.make_async_remote_copy(
            src_ref=source_ref,
            dst_ref=target_ref,
            send_sem=send_sems.at[send_index],
            recv_sem=recv_sems.at[recv_index],
            device_id=device,
            device_id_type=MESH,
        )

    def copy(source_ref, target_ref, device):
        index = take()
        made = describe(source_ref, target_ref, device, index, index)
        made.start()
        sent.append(made)
        return made

    def each(count, step):
        def run(i, carry):
            step(i)
            return carry

        lax.fori_loop(0, count, run, 0)

    def prepare(t):
        lists = (
            (src_in, src_at, edges),
            (rel_ids_in, rel_at, edges),
            (dst_in, target_at, edges),
            (neg_in, target_at + edges, negs),
        )
        for ref, at, count in lists:

            def block(j, ref=ref, at=at):
                row = ref[t : t + 1, pl.ds(pl.multiple_of(j * LANES, LANES), LANES)]
                place = pl.ds(pl.multiple_of(at + j * LANES, LANES), LANES)
                high = (row >> 7).astype(f32)
                low = (row & 127).astype(f32)
                lanes = lax.broadcasted_iota(jnp.int32, (LANES, LANES), 1).astype(f32)
                subs = lax.broadcasted_iota(jnp.int32, (LANES, LANES), 0).astype(f32)
                low_row[t, :, place] = jnp.where(subs == low, 1.0, 0.0).astype(bf16)
                high_row[t, :, place] = jnp.broadcast_to(high, (16, LANES)).astype(bf16)
                column = jnp.broadcast_to(to_column(row.astype(f32)), (LANES, LANES))
                high_c = jnp.floor(column * (1.0 / LANES))
                low_c = column - LANES * high_c
                high_col[t, place, :] = high_c.astype(bf16)
                low_col[t, place, :] = jnp.where(lanes == low_c, 1.0, 0.0).astype(bf16)

            for j in range(count // LANES):
                block(j)

    def level(index, shape):
        return jnp.full(shape, jnp.asarray(index, jnp.int32).astype(f32), f32).astype(bf16)

    def lookup(t, at, count, first_block, n_blocks, table, out, fresh):
        def chunk(i):
            place = pl.ds(pl.multiple_of(at + i * CHUNK, CHUNK), CHUNK)
            high = high_col[t, place, :]
            low = low_col[t, place, :]
            zero = jnp.zeros_like(low)
            matches = jnp.concatenate(
                [
                    jnp.where(high == level(first_block + j, high.shape), low, zero)
                    for j in range(n_blocks)
                ],
                axis=1,
            )
            found = jnp.dot(matches, table[...], preferred_element_type=f32)
            dest = pl.ds(pl.multiple_of(i * CHUNK, CHUNK), CHUNK)
            if fresh:
                out[dest, :] = found
            else:
                out[dest, :] += found

        for i in range(count // CHUNK):
            chunk(i)

    def scatter(t, at, count, first_block, n_blocks, values, store):
        def pair(i):
            high = high_row[t, :, at : at + count]
            low = low_row[t, :, at : at + count]
            one, none = jnp.ones_like(high), jnp.zeros_like(high)
            parts = []
            for j in range(2):
                hit = jnp.where(high == level(first_block + 2 * i + j, high.shape), one, none)
                parts.append(low * jnp.concatenate([hit] * (LANES // 16), axis=0))
            matches = jnp.concatenate(parts, axis=0)
            store(
                pl.ds(pl.multiple_of(i * 2 * LANES, 2 * LANES), 2 * LANES),
                jnp.dot(matches, values[...], preferred_element_type=f32),
            )

        for i in range(n_blocks // 2):
            pair(i)

    def dense(t):
        negatives[...] = target[edges:, :].astype(bf16)
        grad_neg_acc[...] = jnp.zeros_like(grad_neg_acc)

        def chunk(i):
            place = pl.ds(pl.multiple_of(i * CHUNK, CHUNK), CHUNK)
            s_re, s_im = source[place, :half_dim], source[place, half_dim:]
            r_re, r_im = relation[place, :half_dim], relation[place, half_dim:]
            goal = target[place, :]
            product = jnp.concatenate(
                [s_re * r_re - s_im * r_im, s_re * r_im + s_im * r_re], axis=1
            )
            positive = jnp.sum(product * goal, axis=1, keepdims=True)
            rounded = product.astype(bf16)
            product_b[place, :] = rounded
            n_b = negatives[...]
            negative = lax.dot_general(
                rounded, n_b, (((1,), (1,)), ((), ())), preferred_element_type=f32
            )
            g_pos = -1.0 / (1.0 + jnp.exp(positive))
            g_neg = (neg_weight / (1.0 + jnp.exp(-negative))).astype(bf16)
            g_q = g_pos * goal + jnp.dot(g_neg, n_b, preferred_element_type=f32)
            g_re, g_im = g_q[:, :half_dim], g_q[:, half_dim:]
            grad_src[place, :half_dim] = (g_re * r_re + g_im * r_im).astype(bf16)
            grad_src[place, half_dim:] = (g_im * r_re - g_re * r_im).astype(bf16)
            grad_rel[place, :half_dim] = (g_re * s_re + g_im * s_im).astype(bf16)
            grad_rel[place, half_dim:] = (g_im * s_re - g_re * s_im).astype(bf16)
            grad_target[place, :] = (g_pos * product).astype(bf16)
            grad_neg_acc[...] += lax.dot_general(
                g_neg, rounded, (((0,), (0,)), ((), ())), preferred_element_type=f32
            )

        for i in range(edges // CHUNK):
            chunk(i)
        grad_target[edges:, :] = grad_neg_acc[...].astype(bf16)

    def fetch(source_ref, target_ref, index):
        made = pltpu.make_async_copy(source_ref, target_ref, local_sems.at[index])
        made.start()
        return made

    def update_block(i, table_of, state, grad_of, store, state_to):
        place = pl.ds(i * LANES, LANES)
        value, row = adagrad(table_of(place), state[i : i + 1, :], grad_of(place))
        store(place, value)
        state_to[i : i + 1, :] = row

    def reduce_begin(t, at, count, values, to_sib, from_sib, far_sum, own_sum, to_far, from_far):
        copies = []

        def give(i, quarter_index):
            def store(place, value):
                to_sib[t, i, place, :] = value.astype(bf16)

            scatter(t, at, count, quarter_index * blocks, blocks, values, store)
            copies.append(copy(to_sib.at[t, i], from_sib.at[t, i], sibling))

        def keep(quarter_index, total):
            def store(place, value):
                total[place, :] = value

            scatter(t, at, count, quarter_index * blocks, blocks, values, store)

        give(0, far_sib_quarter)
        keep(far_quarter, far_sum)
        copies[0].wait_recv()
        for i in range(PARTS):
            place = pl.ds(i * part, part)
            to_far[t, place, :] = (
                far_sum[place, :] + from_sib[t, 0, place, :].astype(f32)
            ).astype(bf16)
            copies.append(copy(to_far.at[t, place], from_far.at[t, place], far))
        give(1, sib_quarter)
        keep(near_quarter, own_sum)
        return copies[1:]

    def reduce_end(t, copies, own_sum, from_sib, from_far, apply):
        copies[-1].wait_recv()

        def grad_of(place):
            return (
                own_sum[place, :]
                + from_sib[t, 1, place, :].astype(f32)
                + from_far[t, place, :].astype(f32)
            )

        for i in range(PARTS):
            copies[i].wait_recv()
            for j in range(part // LANES):
                apply(i * (part // LANES) + j, grad_of)

    def rel_begin(t):
        pairs = rel_part // LANES
        swaps = []
        for h in range(REL_PARTS):

            def store(place, value, h=h):
                rel_to_sib[t, pl.ds(h * rel_part + place.start, place.size), :] = value.astype(bf16)

            first = ((1 - core) * REL_PARTS + h) * pairs
            scatter(t, rel_at, edges, first, pairs, grad_rel, store)
            span = pl.ds(h * rel_part, rel_part)
            swaps.append(copy(rel_to_sib.at[t, span], rel_from_sib.at[t, span], sibling))
        for h in range(REL_PARTS):

            def keep(place, value, h=h):
                rel_own_sum[pl.ds(h * rel_part + place.start, place.size), :] = value

            scatter(t, rel_at, edges, (core * REL_PARTS + h) * pairs, pairs, grad_rel, keep)
        return swaps

    many = pl.ds(0, (plane - 1) * piece)

    def wait_many(t, h, sem):
        whole = rel_parts.at[t, h, many]
        pltpu.make_async_copy(whole, whole, sem).wait()

    def rel_span(h, index):
        return pl.ds(pl.multiple_of(h * rel_part + index * piece, piece), piece)

    def rel_spread(t, swaps):
        indices = []
        for h in range(REL_PARTS):
            swaps[h].wait_recv()
            index = take()
            indices.append(index)

            def join(place):
                rel_half[t, place, :] = (
                    rel_own_sum[place, :] + rel_from_sib[t, place, :].astype(f32)
                ).astype(bf16)

            def send(k, h=h, index=index):
                place = rel_span(h, lax.rem(at_plane + k + 1, plane))
                join(place)
                describe(
                    rel_half.at[t, place],
                    rel_parts.at[t, h, rows_of(k, piece)],
                    plane_peer(k + 1),
                    index,
                    index,
                ).start()

            each(plane - 1, send)
            join(rel_span(h, at_plane))
        return indices

    def rel_cross(t, h, indices):
        wait_many(t, h, recv_sems.at[indices[h]])
        total = rel_half[t, rel_span(h, at_plane), :].astype(f32)
        for k in range(plane - 1):
            total = total + rel_parts[t, h, k * piece : (k + 1) * piece, :].astype(f32)
        rel_line[t, h, at_line] = total.astype(bf16)
        mine = rel_line.at[t, h, at_line]
        crossed = [copy(mine, mine, line_peer(k)) for k in range(1, line)]
        wait_many(t, h, send_sems.at[indices[h]])
        return crossed

    def rel_gather(t, h, crossed):
        wait_all(crossed)
        total = rel_line[t, h, 0].astype(f32)
        for k in range(1, line):
            total = total + rel_line[t, h, k].astype(f32)
        start = core * half_rows + h * rel_part + at_plane * piece
        place = pl.ds(pl.multiple_of(start, piece), piece)
        rel_full[t, place, :] = total.astype(bf16)
        index = take()

        def send(k):
            mine = rel_full.at[t, place]
            describe(mine, mine, plane_peer(k + 1), index, index).start()

        each(plane - 1, send)
        return index

    def rel_rows_of(which, h):
        start = which * half_rows + h * rel_part
        return pl.ds(pl.multiple_of(start, rel_part), rel_part)

    def rel_back(t, h, index):
        wait_many(t, h, recv_sems.at[index])
        ours = rel_full.at[t, rel_rows_of(core, h)]
        back = copy(ours, ours, sibling)
        wait_many(t, h, send_sems.at[index])
        return back

    def round_relations():
        def block(i):
            place = rows_of(i, CHUNK)
            rel_b[place, :] = rel[place, :].astype(bf16)

        each(rels // CHUNK, block)

    part = quarter // PARTS
    left_part = quarter // LEFT_PARTS

    def part_of(index, i, size):
        return pl.ds(pl.multiple_of(index * quarter + i * size, size), size)

    def left_send(t, i):
        mine = left_all.at[t, part_of(near_quarter, i, left_part)]
        return copy(mine, mine, far), copy(mine, mine, sibling)

    def left_forward(t, far_copies):
        forwarded = []
        for i, made in enumerate(far_copies):
            made.wait_recv()
            theirs = left_all.at[t, part_of(far_quarter, i, left_part)]
            forwarded.append(copy(theirs, theirs, sibling))
        return forwarded

    def right_send(t, i):
        mine = right_own.at[t, pl.ds(i * part, part)]
        return copy(mine, right_all.at[t, part_of(near_quarter, i, part)], following)

    def right_spread(t, rolled):
        to_far, to_sib = [], []
        for i, made in enumerate(rolled):
            made.wait_recv()
            mine = right_all.at[t, part_of(near_quarter, i, part)]
            to_far.append(copy(mine, mine, far))
            to_sib.append(copy(mine, mine, sibling))
        return to_far, to_sib

    def right_forward(t, to_far):
        forwarded = []
        for i, made in enumerate(to_far):
            made.wait_recv()
            theirs = right_all.at[t, part_of(far_quarter, i, part)]
            forwarded.append(copy(theirs, theirs, sibling))
        return forwarded

    def wait_all(copies):
        for made in copies:
            made.wait_recv()

    def look_left(t, index, fresh=False):
        lookup(
            t, src_at, edges, index * blocks, blocks, left_all.at[t, rows_of(index)], source, fresh
        )

    def look_right(t, index, fresh=False):
        lookup(
            t,
            target_at,
            targets,
            index * blocks,
            blocks,
            right_all.at[t, rows_of(index)],
            target,
            fresh,
        )

    def look_relation(t):
        lookup(t, rel_at, edges, 0, rels // LANES, rel_b, relation, True)

    def split_right(t, place, value):
        high = value.astype(bf16)
        right_own[t, place, :] = high
        right_low_own[t, place, :] = (value - high.astype(f32)).astype(bf16)

    def right_rows(t):
        def table_of(place):
            start = pl.multiple_of(near_quarter * quarter + place.start, LANES)
            high = right_all[t, pl.ds(start, place.size), :]
            return high.astype(f32) + right_low[t, place, :].astype(f32)

        return table_of

    def keep_left(place, value):
        left[place, :] = value

    def keep_right(place, value):
        right[place, :] = value

    def keep_rel(place, value):
        rel[place, :] = value
        rel_b[place, :] = value.astype(bf16)

    def left_rows(place):
        return left[place, :]

    def rel_values(place):
        return rel[place, :]

    def rel_grads(place):
        return rel_full[0, place, :].astype(f32)

    def reduce_right(t):
        return reduce_begin(
            t,
            target_at,
            targets,
            grad_target,
            right_to_sib,
            right_from_sib,
            right_far_sum,
            right_own_sum,
            right_to_far,
            right_from_far,
        )

    def reduce_left(t):
        return reduce_begin(
            t,
            src_at,
            edges,
            grad_src,
            left_to_sib,
            left_from_sib,
            left_far_sum,
            left_own_sum,
            left_to_far,
            left_from_far,
        )

    def send_low(t, state):
        return [
            copy(right_low_own.at[t], right_low.at[t], following),
            copy(state, right_state.at[t], following),
        ]

    pairs = (
        (right_in, right),
        (left_in, left),
        (rel_in, rel),
        (rel_rows, rel_ids_in),
        (src_rows, src_in),
        (dst_rows, dst_in),
        (neg_rows, neg_in),
        (right_state_in, right_state_first),
        (left_state_in, left_state),
        (rel_state_in, rel_state),
    )
    barrier = pltpu.get_barrier_semaphore()
    greeted = [sibling, following, preceding]
    greeted += [line_peer(k) for k in range(1, line)]
    for device in greeted:
        pl.semaphore_signal(barrier, inc=1, device_id=device, device_id_type=MESH)

    def greet(k):
        pl.semaphore_signal(barrier, inc=1, device_id=plane_peer(k + 1), device_id_type=MESH)

    each(plane - 1, greet)
    fetched = [fetch(a, b, i) for i, (a, b) in enumerate(pairs)]
    fetched[0].wait()
    split_right(0, pl.ds(0, quarter), right[...])
    fetched[1].wait()
    left_all[0, rows_of(near_quarter), :] = left[...].astype(bf16)
    pl.semaphore_wait(barrier, len(greeted) + plane - 1)

    rolled = [right_send(0, i) for i in range(PARTS)]
    for made in rolled[: PARTS // 2]:
        made.wait_send()
    early = rolled[: PARTS // 2]
    left_far, left_sib = zip(*[left_send(0, i) for i in range(LEFT_PARTS)])
    for made in fetched[2:]:
        made.wait()
    round_relations()
    prepare(0)
    look_left(0, near_quarter, True)
    wait_all(left_sib)
    look_left(0, sib_quarter)
    right_far, right_sib = right_spread(0, rolled)
    left_far_sib = left_forward(0, left_far)
    look_relation(0)
    look_left(0, far_quarter)
    look_right(0, near_quarter, True)
    wait_all(left_far_sib)
    look_left(0, far_sib_quarter)
    wait_all(right_sib)
    look_right(0, sib_quarter)
    prepare(1)
    right_far_sib = right_forward(0, right_far)
    lows = send_low(0, right_state_first)
    look_right(0, far_quarter)
    wait_all(right_far_sib)
    look_right(0, far_sib_quarter)
    dense(0)

    right_copies = reduce_right(0)
    spread = rel_spread(0, rel_begin(0))
    left_copies = reduce_left(0)
    wait_all(lows)
    rolled = []

    def next_right(i, grad_of):
        update_block(
            i,
            right_rows(0),
            right_state.at[0],
            grad_of,
            functools.partial(split_right, 1),
            right_state_next,
        )
        if (i + 1) % (part // LANES) == 0:
            rolled.append(right_send(1, i // (part // LANES)))

    reduce_end(0, right_copies, right_own_sum, right_from_sib, right_from_far, next_right)
    crossed = [rel_cross(0, 0, spread)]
    left_sent = []

    def next_left(i, grad_of):
        update_block(i, left_rows, left_state, grad_of, keep_left, left_state)
        block = pl.ds(i * LANES, LANES)
        left_all[1, part_of(near_quarter, i, LANES), :] = left[block, :].astype(bf16)
        if (i + 1) % (left_part // LANES) == 0:
            left_sent.append(left_send(1, i // (left_part // LANES)))

    reduce_end(0, left_copies, left_own_sum, left_from_sib, left_from_far, next_left)
    left_far, left_sib = zip(*left_sent)
    crossed += [rel_cross(0, h, spread) for h in range(1, REL_PARTS)]
    gathered = [rel_gather(0, 0, crossed[0])]
    right_far, right_sib = right_spread(1, rolled)
    gathered += [rel_gather(0, h, crossed[h]) for h in range(1, REL_PARTS)]
    look_left(1, near_quarter, True)
    wait_all(left_sib)
    look_left(1, sib_quarter)
    left_far_sib = left_forward(1, left_far)
    back = [rel_back(0, h, gathered[h]) for h in range(REL_PARTS)]
    look_left(1, far_quarter)
    wait_all(left_far_sib)
    look_left(1, far_sib_quarter)
    wait_all(back)
    for i in range(rels // LANES):
        update_block(i, rel_values, rel_state, rel_grads, keep_rel, rel_state)
    rel_written = [fetch(rel, rel_out, 0), fetch(rel_state, rel_state_out, 1)]
    look_relation(1)
    look_right(1, near_quarter, True)
    wait_all(right_sib)
    look_right(1, sib_quarter)
    right_far_sib = right_forward(1, right_far)
    lows = send_low(1, right_state_next)
    look_right(1, far_quarter)
    wait_all(right_far_sib)
    look_right(1, far_sib_quarter)
    dense(1)

    spread = rel_spread(1, rel_begin(1))
    right_copies = reduce_right(1)
    crossed = [rel_cross(1, h, spread) for h in range(REL_PARTS)]
    gathered = [rel_gather(1, h, crossed[h]) for h in range(REL_PARTS)]
    left_copies = reduce_left(1)
    wait_all(lows)

    def last_right(i, grad_of):
        update_block(
            i, right_rows(1), right_state.at[1], grad_of, keep_right, right_state_last
        )

    reduce_end(1, right_copies, right_own_sum, right_from_sib, right_from_far, last_right)
    written = [fetch(right, right_out, 2), fetch(right_state_last, right_state_out, 3)]

    def last_left(i, grad_of):
        update_block(i, left_rows, left_state, grad_of, keep_left, left_state)

    reduce_end(1, left_copies, left_own_sum, left_from_sib, left_from_far, last_left)
    written += [fetch(left, left_out, 4), fetch(left_state, left_state_out, 5)]
    back = []
    for h in range(REL_PARTS):
        back.append(rel_back(1, h, gathered[h]))
        ours = rel_rows_of(core, h)
        written.append(fetch(rel_full.at[1, ours], rel_grad_out.at[ours], 6 + 2 * h))
    for h in range(REL_PARTS):
        back[h].wait_recv()
        theirs = rel_rows_of(1 - core, h)
        written.append(fetch(rel_full.at[1, theirs], rel_grad_out.at[theirs], 7 + 2 * h))
    for made in rel_written + written:
        made.wait()
    for made in sent:
        if not any(made is r for r in early):
            made.wait_send()


def finish(left, left_state, right, right_state, rel, rel_state, rel_grad, *results):
    left_out, left_state_out, right_out, right_state_out, rel_out, rel_state_out = results
    left_out[...] = left[...]
    right_out[...] = right[...]
    left_state_out[...] = left_state[...]
    right_state_out[...] = right_state[...]
    count = rel.shape[0] // LANES
    first = pl.program_id(0) * count
    for i in range(count):
        place = pl.ds(i * LANES, LANES)
        value, row = adagrad(
            rel[place, :], rel_state[pl.ds(first + i, 1), :], rel_grad[place, :].astype(jnp.float32)
        )
        rel_out[place, :] = value
        rel_state_out[pl.ds(first + i, 1), :] = row


def local(
    left_table,
    left_state,
    right_table,
    right_state,
    relations,
    relation_state,
    src_rows,
    dst_rows,
    rel_ids,
    neg_rows,
):
    quarter, width = left_table.shape
    edges = src_rows.shape[1]
    negs = neg_rows.shape[1]
    rels = relations.shape[0]
    slab = quarter * lax.axis_size("edge")
    indices = 3 * edges + negs
    targets = edges + negs
    f32, bf16 = jnp.float32, jnp.bfloat16
    state_shape = (quarter // LANES, LANES)
    rel_state_shape = (rels // LANES, LANES)

    line = 4
    piece = rels // 2 // (lax.axis_size("dom") // 2) // REL_PARTS

    def vmem(shape, kind):
        return pltpu.VMEM(shape, kind)

    half_rows = rels // 2
    results = pl.pallas_call(
        functools.partial(body, lax.axis_size("dom")),
        out_shape=(
            jax.ShapeDtypeStruct((quarter, width), f32),
            jax.ShapeDtypeStruct(state_shape, f32),
            jax.ShapeDtypeStruct((quarter, width), f32),
            jax.ShapeDtypeStruct(state_shape, f32),
            jax.ShapeDtypeStruct((rels, width), f32),
            jax.ShapeDtypeStruct(rel_state_shape, f32),
            jax.ShapeDtypeStruct((rels, width), bf16),
        ),
        in_specs=[pl.BlockSpec(memory_space=pl.ANY)] * 10,
        out_specs=tuple([pl.BlockSpec(memory_space=pl.ANY)] * 7),
        scratch_shapes=[
            vmem((quarter, width), f32),
            vmem(state_shape, f32),
            vmem((quarter, width), f32),
            vmem(state_shape, f32),
            vmem((rels, width), f32),
            vmem(rel_state_shape, f32),
            vmem(src_rows.shape, jnp.int32),
            vmem(dst_rows.shape, jnp.int32),
            vmem(rel_ids.shape, jnp.int32),
            vmem(neg_rows.shape, jnp.int32),
            vmem((STEPS, indices, LANES), bf16),
            vmem((STEPS, indices, LANES), bf16),
            vmem((STEPS, 16, indices), bf16),
            vmem((STEPS, LANES, indices), bf16),
            vmem((rels, width), bf16),
            vmem((edges, width), f32),
            vmem((targets, width), f32),
            vmem((edges, width), f32),
            vmem((negs, width), bf16),
            vmem((edges, width), bf16),
            vmem((edges, width), bf16),
            vmem((edges, width), bf16),
            vmem((targets, width), bf16),
            vmem((negs, width), f32),
            vmem((STEPS, slab, width), bf16),
            vmem((STEPS, slab, width), bf16),
            vmem((STEPS, quarter, width), bf16),
            vmem((STEPS, quarter, width), bf16),
            vmem((STEPS, quarter, width), bf16),
            vmem((STEPS,) + state_shape, f32),
            vmem(state_shape, f32),
            vmem(state_shape, f32),
            vmem((quarter, width), f32),
            vmem((quarter, width), f32),
            vmem((quarter, width), f32),
            vmem((quarter, width), f32),
            vmem((half_rows, width), f32),
            vmem((STEPS, 2, quarter, width), bf16),
            vmem((STEPS, 2, quarter, width), bf16),
            vmem((STEPS, quarter, width), bf16),
            vmem((STEPS, quarter, width), bf16),
            vmem((STEPS, 2, quarter, width), bf16),
            vmem((STEPS, 2, quarter, width), bf16),
            vmem((STEPS, quarter, width), bf16),
            vmem((STEPS, quarter, width), bf16),
            vmem((STEPS, half_rows, width), bf16),
            vmem((STEPS, half_rows, width), bf16),
            vmem((STEPS, half_rows, width), bf16),
            vmem((STEPS, REL_PARTS, half_rows // REL_PARTS, width), bf16),
            vmem((STEPS, REL_PARTS, line, piece, width), bf16),
            vmem((STEPS, rels, width), bf16),
            pltpu.SemaphoreType.DMA((160,)),
            pltpu.SemaphoreType.DMA((160,)),
            pltpu.SemaphoreType.DMA((10,)),
        ],
        name="buckets",
        compiler_params=pltpu.CompilerParams(
            collective_id=0, has_side_effects=True, vmem_limit_bytes=56 << 20
        ),
    )(
        left_table,
        left_state.reshape(state_shape),
        right_table,
        right_state.reshape(state_shape),
        relations,
        relation_state.reshape(rel_state_shape),
        src_rows,
        dst_rows,
        rel_ids,
        neg_rows,
    )
    rows = pl.BlockSpec((quarter // FINISH, width), lambda i: (i, 0))
    states = pl.BlockSpec(state_shape, lambda i: (0, 0))
    rel_rows = pl.BlockSpec((rels // FINISH, width), lambda i: (i, 0))
    rel_states = pl.BlockSpec(rel_state_shape, lambda i: (0, 0))
    blocks = (rows, states, rows, states, rel_rows, rel_states)
    left, left_s, right, right_s, rel, rel_s = pl.pallas_call(
        finish,
        grid=(FINISH,),
        out_shape=tuple(jax.ShapeDtypeStruct(r.shape, f32) for r in results[:6]),
        in_specs=list(blocks) + [rel_rows],
        out_specs=blocks,
        name="finish",
        compiler_params=pltpu.CompilerParams(vmem_limit_bytes=56 << 20),
    )(*results)
    return (left, left_s.reshape(-1), right, right_s.reshape(-1), rel, rel_s.reshape(-1))


def solution(mesh):
    placed = (
        P(("dom", "edge"), None),
        P(("dom", "edge")),
        P(("dom", "edge"), None),
        P(("dom", "edge")),
        P(),
        P(),
        P(None, ("dom", "edge")),
        P(None, ("dom", "edge")),
        P(None, ("dom", "edge")),
        P(None, ("dom", "edge")),
    )
    return jax.shard_map(
        local,
        mesh=mesh,
        in_specs=placed,
        out_specs=(
            P(("dom", "edge"), None),
            P(("dom", "edge")),
            P(("dom", "edge"), None),
            P(("dom", "edge")),
            P(),
            P(),
        ),
        check_vma=False,
    )
```
